32 devices in a mesh: groups: 2 (over y), sec: 2 (over x), row: 4 (over z), col: 2 (over core).
Axes of the slice: x: 2, y: 2, z: 4, core: 2. Of those that a mesh axis runs over, the one named last changes fastest.
Arguments:
- factors: bfloat16 [4, 2048, 2048], P(('groups', 'sec'), 'row', 'col'), parts along dimension 0, may hold values from -0.125 to 0.125
- inverses: bfloat16 [4, 2048, 2048], P(('groups', 'sec'), 'row', 'col'), parts along dimension 0, may hold values from -1.4 to 1.4, as said below
- sigma_end: float32 [4096, 2048], P(('groups', 'row'), 'col'), parts along dimension 0, may hold values from -1 to 6, as said below
Outputs:
- variance: float32 [4, 2048, 2048], P(('groups', 'sec'), 'row', 'col'), parts along dimension 0
The draws below stay inside these ranges and needn't reach their ends.
There are 2 independent parts, one for each index of `groups`. The reference program is written for one: setup_inputs(seed, part) draws one part's arguments, and reference() takes and returns one part's arrays. A program takes and returns all parts, laid end to end along the dimension named above; each array names one. Nothing has to cross between parts.
Inputs may be any that keep to these rules, and one draw needn't show every extreme that they name: inverses[t] is lower triangular; its diagonal entries lie in 0.6 to 1.4. sigma_end is symmetric with diagonal entries in 2.5 to 6.
All inputs are finite; a program needn't handle non-finite values.
Results may differ from the reference program's by a relative error of at most 0.011.
Values may be sent and summed in bfloat16 or wider, within the bound.
No kernel may reach another device: no remote copies, remote signals or barrier semaphores. Data moves between devices by JAX's collectives and lax.ppermute only.
A program may use at most 64 MiB of HBM per device.

```python
import math
import jax
import jax.numpy as jnp
from jax import lax

B = 2048
STEPS = 2


def draw_inverses(key, part):
    first_key, second_key = jax.random.split(jax.random.fold_in(key, 7))
    shape = (STEPS, B, B)
    below = jnp.clip(jax.random.normal(first_key, shape, jnp.float32) * 0.7, -2.8, 2.8)
    below = below / math.sqrt(B)
    diag_values = jax.random.uniform(second_key, (STEPS, 1, B), jnp.float32, 0.6, 1.4)
    row_ids = lax.broadcasted_iota(jnp.int32, (1, B, B), 1)
    col_ids = lax.broadcasted_iota(jnp.int32, (1, B, B), 2)
    lower = jnp.where(col_ids < row_ids, below, 0.0) + jnp.where(col_ids == row_ids, diag_values, 0.0)
    return lower.astype(jnp.bfloat16)


def draw_sigma_end(key, part):
    first_key, second_key = jax.random.split(jax.random.fold_in(key, 13))
    raw = jnp.clip(jax.random.normal(first_key, (B, B), jnp.float32), -4.0, 4.0)
    raw = raw / math.sqrt(B)
    symmetric = 0.5 * (raw + raw.T)
    diag_values = jax.random.uniform(second_key, (1, B), jnp.float32, 2.5, 6.0)
    row_ids = lax.broadcasted_iota(jnp.int32, (B, B), 0)
    col_ids = lax.broadcasted_iota(jnp.int32, (B, B), 1)
    return jnp.where(row_ids == col_ids, diag_values, symmetric).astype(jnp.float32)


def block_scale(stream_key, shape, cuts, smallest, largest):
    def one(dim, blocks):
        draws = jax.random.uniform(jax.random.fold_in(jax.random.fold_in(stream_key, 6), dim), (blocks,), jnp.float32, smallest / len(cuts), largest / len(cuts))
        return jnp.repeat(jnp.exp(draws), shape[dim] // blocks).reshape((-1,) + (1,) * (len(shape) - dim - 1))

    level = one(*cuts[0])
    for cut in cuts[1:]:
        level = level * one(*cut)
    return level


def noise(rng, dims, width, bound, shards=(), dtype=jnp.bfloat16):
    array = width * jax.random.normal(rng, dims, jnp.float32)
    if shards:
        array = array * block_scale(rng, dims, shards, -0.22, 0.18)
    return jnp.clip(array, -bound, bound).astype(dtype)


def setup_inputs(seed: int = 0, part: int = 0) -> dict:
    arg_keys = jax.random.split(jax.random.key(seed), 4)
    part_splits = jax.random.split(jax.random.fold_in(arg_keys[3], part), 4)
    factors = noise(part_splits[0], (STEPS, B, B), B ** -0.5, 0.125, ((0, 2), (1, 4), (2, 2)))
    inverses = draw_inverses(jax.random.fold_in(jax.random.fold_in(arg_keys[3], part), 71), part)
    sigma_end = draw_sigma_end(jax.random.fold_in(jax.random.fold_in(arg_keys[3], part), 71), part)
    return dict(factors=factors, inverses=inverses, sigma_end=sigma_end)


def reference(factors, inverses, sigma_end):
    count = factors.shape[0]
    state = sigma_end
    produced = []
    for position in range(count - 1, -1, -1):
        inverse_now = inverses[position]
        diag_term = jnp.dot(inverse_now.T, inverse_now, preferred_element_type=jnp.float32)
        state_low = state.astype(jnp.bfloat16)
        image = jnp.dot(state_low, factors[position], preferred_element_type=jnp.float32).astype(jnp.bfloat16)
        result = diag_term + jnp.dot(factors[position].T, image, preferred_element_type=jnp.float32)
        produced.append(result)
        state = result
    return jnp.stack(produced[::-1])
```

```python
import jax
import jax.numpy as jnp
from jax import lax
from jax.sharding import PartitionSpec as P

CHUNKS = 2


def transposed_dot(left, right):
    return lax.dot_general(
        left, right, (((0,), (0,)), ((), ())), preferred_element_type=jnp.float32
    )


def dot(left, right):
    return jnp.dot(left, right, preferred_element_type=jnp.float32)


def exchanged(value, axis, steps):
    count = lax.axis_size(axis)
    return lax.ppermute(value, axis, [(i, (i + steps) % count) for i in range(count)])


def both_halves(own):
    col_size = lax.axis_size("col")
    col_index = lax.axis_index("col")
    pieces = [own] + [exchanged(own, "col", k) for k in range(1, col_size)]
    ordered = []
    for c in range(col_size):
        piece = pieces[0]
        for k in range(1, col_size):
            piece = jnp.where((col_index - k) % col_size == c, pieces[k], piece)
        ordered.append(piece)
    return jnp.concatenate(ordered, axis=-1)


def spread_over_sections(tile, width):
    sec_size = lax.axis_size("sec")
    sec_index = lax.axis_index("sec")

    def panel(array, offset):
        first = (sec_index + offset) % sec_size * width
        return lax.dynamic_slice_in_dim(array, first, width, 1)

    arrived = [(panel(tile, 0), tile)]
    for k in range(1, sec_size):
        pieces = [
            exchanged(panel(tile, (k + j) % sec_size), "sec", k) for j in range(sec_size)
        ]
        whole = jnp.zeros_like(tile)
        for j in range(sec_size):
            first = (sec_index + j) % sec_size * width
            whole = lax.dynamic_update_slice_in_dim(whole, pieces[j], first, 1)
        arrived.append((pieces[0], whole))

    panels, tiles = [], []
    for step in range(sec_size):
        chosen_panel, chosen_tile = arrived[0]
        for k in range(1, sec_size):
            here = (sec_index - k) % sec_size == step
            chosen_panel = jnp.where(here, arrived[k][0], chosen_panel)
            chosen_tile = jnp.where(here, arrived[k][1], chosen_tile)
        panels.append(chosen_panel)
        tiles.append(chosen_tile)
    return panels, tiles


def scattered_sum(partial, rows):
    row_size = lax.axis_size("row")
    row_index = lax.axis_index("row")

    def block(number):
        number = jnp.clip(number, 0, row_size - 1)
        return lax.dynamic_slice_in_dim(partial, number * rows, rows, 0)

    up = down = None
    for slot in range(row_size - 1):
        up_block = block(row_size - 1 - slot + row_index)
        down_block = block(row_index + slot - (row_size - 1))
        if slot:
            up_block = up_block + up
            down_block = down_block + down
        up = lax.ppermute(
            up_block.astype(jnp.bfloat16), "row", [(i, i + 1) for i in range(slot + 1)]
        ).astype(jnp.float32)
        down = lax.ppermute(
            down_block.astype(jnp.bfloat16),
            "row",
            [(i, i - 1) for i in range(row_size - 1 - slot, row_size)],
        ).astype(jnp.float32)
    return block(row_index) + up + down


def local(factors, inverses, sigma_end):
    row_size = lax.axis_size("row")
    sec_size = lax.axis_size("sec")
    sec_index = lax.axis_index("sec")
    step_count, rows, cols = factors.shape
    assert step_count == 1
    width = cols // sec_size
    chunk = width // CHUNKS

    factor_panels, factor_tiles = spread_over_sections(factors[0], width)
    gathered = {}
    for step in reversed(range(sec_size)):
        for part in range(CHUNKS):
            piece = factor_panels[step][:, part * chunk : (part + 1) * chunk]
            gathered[step, part] = lax.all_gather(piece, "row", axis=0, tiled=True)
    inverse_panels, inverse_tiles = spread_over_sections(inverses[0], width)

    state = both_halves(sigma_end.astype(jnp.bfloat16))
    output = jnp.zeros((rows, cols), jnp.float32)
    for step in reversed(range(sec_size)):
        factor_rows = both_halves(factor_tiles[step])
        inverse_rows = both_halves(inverse_tiles[step])
        summed = []
        for part in range(CHUNKS):
            inverse_piece = inverse_panels[step][:, part * chunk : (part + 1) * chunk]
            diagonal = transposed_dot(inverse_rows, inverse_piece)
            image = dot(state, gathered[step, part]).astype(jnp.bfloat16)
            partial = diagonal + transposed_dot(factor_rows, image)
            summed.append(scattered_sum(partial, rows).astype(jnp.bfloat16))
        panel = jnp.concatenate(summed, axis=1)
        tile = jnp.zeros((rows, cols), jnp.bfloat16)
        tile = lax.dynamic_update_slice_in_dim(tile, panel, sec_index * width, 1)
        for k in range(1, sec_size):
            other = exchanged(panel, "sec", k)
            first = (sec_index - k) % sec_size * width
            tile = lax.dynamic_update_slice_in_dim(tile, other, first, 1)
        output = jnp.where(sec_index == step, tile.astype(jnp.float32), output)
        if step:
            state = both_halves(tile)
    return output[None]


def solution(mesh):
    in_specs = (
        P(("groups", "sec"), "row", "col"),
        P(("groups", "sec"), "row", "col"),
        P(("groups", "row"), "col"),
    )
    out_specs = P(("groups", "sec"), "row", "col")
    return jax.shard_map(local, mesh=mesh, in_specs=in_specs, out_specs=out_specs, check_vma=False)
```

```python
import functools

import jax
import jax.numpy as jnp
from jax import lax
from jax.experimental import pallas as pl
from jax.experimental.pallas import tpu as pltpu
from jax.sharding import PartitionSpec as P

CHUNKS = 2
ANY = pl.BlockSpec(memory_space=pl.ANY)
VMEM = pl.BlockSpec(memory_space=pltpu.VMEM)
PARAMS = pltpu.CompilerParams(vmem_limit_bytes=32 * 1024 * 1024)


def exchanged(value, axis, steps):
    count = lax.axis_size(axis)
    return lax.ppermute(value, axis, [(i, (i + steps) % count) for i in range(count)])


class Sizes:
    def __init__(self, rows, cols):
        self.row = lax.axis_size("row")
        self.sec = lax.axis_size("sec")
        self.col = lax.axis_size("col")
        self.rows = rows
        self.cols = cols
        self.order = cols * self.col
        self.width = cols // self.sec
        self.chunk = self.width // CHUNKS
        self.per_tile = self.row // self.col


def chosen_copies(sizes, step, tiles, target, sems):
    sec_index, col_index = lax.axis_index("sec"), lax.axis_index("col")
    copies = []
    for kc in range(sizes.col):
        place = lax.rem(col_index - kc + sizes.col, sizes.col)
        for kx in range(sizes.sec):
            copy = pltpu.make_async_copy(tiles[kx][kc], target.at[place], sems.at[kc])
            wanted = lax.rem(sec_index - kx + sizes.sec, sizes.sec) == step
            copies.append((wanted, copy))
    return copies


def start_all(copies):
    for wanted, copy in copies:
        pl.when(wanted)(copy.start)


def wait_all(copies):
    for wanted, copy in copies:
        pl.when(wanted)(copy.wait)


def nested(refs, sizes):
    return [refs[kx * sizes.col : (kx + 1) * sizes.col] for kx in range(sizes.sec)]


def diagonal_kernel(sizes, step, *refs):
    count = sizes.sec * sizes.col
    tiles, (out, held, sems) = nested(refs[:count], sizes), refs[count:]
    copies = chosen_copies(sizes, step, tiles, held, sems)
    start_all(copies)
    wait_all(copies)
    first = lax.axis_index("sec") * sizes.width
    for k in range(CHUNKS):
        begin = pl.multiple_of(first + k * sizes.chunk, sizes.chunk)
        left = held[lax.axis_index("col"), :, pl.ds(begin, sizes.chunk)].T
        for d in range(sizes.row):
            h, i = divmod(d, sizes.per_tile)
            right = held[h, :, i * sizes.rows : (i + 1) * sizes.rows]
            out[k, d] = jnp.dot(left, right, preferred_element_type=jnp.float32)


def diagonal(sizes, step, tiles):
    flat = [tile for per_section in tiles for tile in per_section]
    shape = (CHUNKS, sizes.row, sizes.chunk, sizes.rows)
    return pl.pallas_call(
        functools.partial(diagonal_kernel, sizes, step),
        out_shape=jax.ShapeDtypeStruct(shape, jnp.float32),
        in_specs=[ANY] * len(flat),
        out_specs=VMEM,
        scratch_shapes=[
            pltpu.VMEM((sizes.col, sizes.rows, sizes.cols), jnp.bfloat16),
            pltpu.SemaphoreType.DMA((sizes.col,)),
        ],
        compiler_params=PARAMS,
        cost_estimate=pl.CostEstimate(
            flops=2 * sizes.rows * sizes.width * sizes.order,
            bytes_accessed=2 * sizes.rows * sizes.order + 4 * sizes.width * sizes.order,
            transcendentals=0,
        ),
        name="diagonal",
    )(*flat)


def panel_kernel(sizes, step, offset, own, *refs):
    *sent, out, held, sem = refs
    sec_index = lax.axis_index("sec")
    count = out.shape[0]
    begin = pl.multiple_of(sec_index * sizes.width + offset, sizes.chunk)
    copies = [(sec_index == step, pltpu.make_async_copy(own.at[:, pl.ds(begin, count)], held, sem))]
    per_section = len(sent) // (sizes.sec - 1)
    for kx in range(1, sizes.sec):
        wanted = lax.rem(sec_index - kx + sizes.sec, sizes.sec) == step
        pieces = sent[(kx - 1) * per_section : kx * per_section]
        height = count // per_section
        for k, piece in enumerate(pieces):
            target = held.at[:, k * height : (k + 1) * height]
            copies.append((wanted, pltpu.make_async_copy(piece, target, sem)))
    start_all(copies)
    wait_all(copies)
    out[...] = held[...].T


def transposed_panel(sizes, step, own, sent, part=None):
    count = sizes.width if part is None else sizes.chunk
    offset = 0 if part is None else part * sizes.chunk
    flat = [piece for pieces in sent for piece in pieces]
    return pl.pallas_call(
        functools.partial(panel_kernel, sizes, step, offset),
        out_shape=jax.ShapeDtypeStruct((count, sizes.rows), jnp.bfloat16),
        in_specs=[ANY] * (1 + len(flat)),
        out_specs=VMEM,
        scratch_shapes=[
            pltpu.VMEM((sizes.rows, count), jnp.bfloat16),
            pltpu.SemaphoreType.DMA,
        ],
        compiler_params=PARAMS,
        name="panel",
    )(own, *flat)


def products_kernel(sizes, step, part, block_shifts, state_places, *refs):
    n_blocks, n_states, n_tiles = len(block_shifts), len(state_places), sizes.sec * sizes.col
    blocks, refs = refs[:n_blocks], refs[n_blocks:]
    states, refs = refs[:n_states], refs[n_states:]
    tiles, refs = nested(refs[:n_tiles], sizes), refs[n_tiles:]
    diagonals, out, state, rows, added, tile_sems, state_sems, added_sem = refs
    row_index, sec_index, col_index = (lax.axis_index(a) for a in ("row", "sec", "col"))

    state_copies = []
    for number, (kx, kc, offset) in enumerate(state_places):
        first = lax.rem(col_index - kc + sizes.col, sizes.col) * sizes.cols + offset
        if kx is not None:
            first = first + lax.rem(sec_index - kx + sizes.sec, sizes.sec) * sizes.width
        height = states[number].shape[0]
        place = state.at[pl.ds(pl.multiple_of(first, height), height)]
        state_copies.append(pltpu.make_async_copy(states[number], place, state_sems.at[number]))
    for copy in state_copies:
        copy.start()
    tile_copies = chosen_copies(sizes, step, tiles, rows, tile_sems)
    start_all(tile_copies)
    added_copy = pltpu.make_async_copy(diagonals.at[part], added, added_sem)
    added_copy.start()
    for copy in state_copies:
        copy.wait()

    out[0] = jnp.zeros((sizes.chunk, sizes.rows), jnp.float32)
    for number, shift in enumerate(block_shifts):
        def accumulate(block, q):
            first = pl.multiple_of(q * sizes.rows, sizes.rows)
            out[0] += jnp.dot(
                block, state[pl.ds(first, sizes.rows)], preferred_element_type=jnp.float32
            )

        if shift is None:
            for q in range(sizes.row):
                accumulate(blocks[number][q, part * sizes.chunk : (part + 1) * sizes.chunk], q)
        else:
            q = row_index + shift
            pl.when((q >= 0) & (q < sizes.row))(
                functools.partial(lambda ref, q: accumulate(ref[...], q), blocks[number], q)
            )
    image = out[0].astype(jnp.bfloat16)
    wait_all(tile_copies)
    added_copy.wait()
    for d in range(sizes.row):
        h, i = divmod(d, sizes.per_tile)
        right = rows[h, :, i * sizes.rows : (i + 1) * sizes.rows]
        out[d] = jnp.dot(image, right, preferred_element_type=jnp.float32) + added[d]


def products(sizes, step, part, blocks, states, tiles, diagonals):
    flat = [tile for per_section in tiles for tile in per_section]
    shape = (sizes.row, sizes.chunk, sizes.rows)
    return pl.pallas_call(
        functools.partial(
            products_kernel, sizes, step, part, [b[0] for b in blocks], [s[0] for s in states]
        ),
        out_shape=jax.ShapeDtypeStruct(shape, jnp.float32),
        in_specs=[VMEM] * len(blocks) + [ANY] * (len(states) + len(flat) + 1),
        out_specs=VMEM,
        scratch_shapes=[
            pltpu.VMEM((sizes.order, sizes.rows), jnp.bfloat16),
            pltpu.VMEM((sizes.col, sizes.rows, sizes.cols), jnp.bfloat16),
            pltpu.VMEM(shape, jnp.float32),
            pltpu.SemaphoreType.DMA((sizes.col,)),
            pltpu.SemaphoreType.DMA((len(states),)),
            pltpu.SemaphoreType.DMA,
        ],
        compiler_params=PARAMS,
        cost_estimate=pl.CostEstimate(
            flops=4 * sizes.rows * sizes.chunk * sizes.order,
            bytes_accessed=4 * sizes.rows * sizes.order + 10 * sizes.chunk * sizes.order,
            transcendentals=0,
        ),
        name="products",
    )(*[b[1] for b in blocks], *[s[1] for s in states], *flat, diagonals)


def output_kernel(sizes, *refs):
    per_step = sizes.sec * CHUNKS
    out = refs[-1]
    sec_index = lax.axis_index("sec")
    for step in range(sizes.sec):

        @pl.when(sec_index == step)
        def _():
            for kx in range(sizes.sec):
                for k in range(CHUNKS):
                    piece = refs[step * per_step + kx * CHUNKS + k][...]
                    first = lax.rem(sec_index - kx + sizes.sec, sizes.sec) * sizes.width
                    begin = pl.multiple_of(first + k * sizes.chunk, sizes.chunk)
                    out[:, pl.ds(begin, sizes.chunk)] = piece.astype(jnp.float32).T


def output(sizes, pieces):
    return pl.pallas_call(
        functools.partial(output_kernel, sizes),
        out_shape=jax.ShapeDtypeStruct((sizes.rows, sizes.cols), jnp.float32),
        in_specs=[VMEM] * len(pieces),
        out_specs=VMEM,
        compiler_params=PARAMS,
        name="output",
    )(*pieces)


def neighbours_gathered(sizes, block):
    up = down = block
    found = [(0, block)]
    for slot in range(sizes.row - 1):
        up = lax.ppermute(up, "row", [(i, i + 1) for i in range(slot, sizes.row - 1)])
        down = lax.ppermute(down, "row", [(i, i - 1) for i in range(1, sizes.row - slot)])
        found += [(-1 - slot, up), (1 + slot, down)]
    return found


def scattered_sum(sizes, partial):
    row_index = lax.axis_index("row")

    def block(number):
        number = jnp.clip(number, 0, sizes.row - 1)
        return lax.dynamic_index_in_dim(partial, number, 0, keepdims=False)

    up = down = None
    last = sizes.row - 1
    for slot in range(last):
        up_block = block(last - slot + row_index)
        down_block = block(row_index + slot - last)
        if slot:
            up_block = up_block + up.astype(jnp.float32)
            down_block = down_block + down.astype(jnp.float32)
        up = lax.ppermute(
            up_block.astype(jnp.bfloat16), "row", [(i, i + 1) for i in range(slot + 1)]
        )
        down = lax.ppermute(
            down_block.astype(jnp.bfloat16), "row", [(i, i - 1) for i in range(last - slot, last + 1)]
        )
    total = block(row_index) + up.astype(jnp.float32) + down.astype(jnp.float32)
    return total.astype(jnp.bfloat16)


def local(factors, inverses, sigma_end):
    step_count, rows, cols = factors.shape
    assert step_count == 1
    sizes = Sizes(rows, cols)
    sec_size, col_size, width, chunk = sizes.sec, sizes.col, sizes.width, sizes.chunk
    sec_index = lax.axis_index("sec")

    def panel(tile, offset, part=None):
        first = (sec_index + offset) % sec_size * width
        if part is None:
            return lax.dynamic_slice_in_dim(tile, first, width, 1)
        return lax.dynamic_slice_in_dim(tile, first + part * chunk, chunk, 1)

    factor, inverse = factors[0], inverses[0]

    arrived_chunks = [None]
    for kx in range(1, sec_size):
        arrived_chunks.append(
            [exchanged(panel(factor, kx, part), "sec", kx) for part in range(CHUNKS)]
        )

    factor_blocks = {}
    last = sec_size - 1
    for part in range(CHUNKS):
        sent = [[chunks[part]] for chunks in arrived_chunks[1:]]
        block = transposed_panel(sizes, last, factor, sent, part)
        factor_blocks[last, part] = neighbours_gathered(sizes, block)
    for step in reversed(range(last)):
        block = transposed_panel(sizes, step, factor, arrived_chunks[1:])
        whole = lax.all_gather(block, "row", axis=0)
        for part in range(CHUNKS):
            factor_blocks[step, part] = [(None, whole)]

    def tiles_over_sections(tile, first_chunks):
        found = [tile]
        for kx in range(1, sec_size):
            whole = jnp.zeros_like(tile)
            for j in range(sec_size):
                if j == 0 and first_chunks is not None:
                    piece = jnp.concatenate(first_chunks[kx], axis=1)
                else:
                    piece = exchanged(panel(tile, kx + j), "sec", kx)
                first = (sec_index + j) % sec_size * width
                whole = lax.dynamic_update_slice_in_dim(whole, piece, first, 1)
            found.append(whole)
        return found

    def over_columns(value):
        return [value] + [exchanged(value, "col", kc) for kc in range(1, col_size)]

    state_pieces = [
        ((None, kc, 0), piece)
        for kc, piece in enumerate(over_columns(sigma_end.astype(jnp.bfloat16).T))
    ]
    factor_tiles = [over_columns(tile) for tile in tiles_over_sections(factor, arrived_chunks)]
    inverse_tiles = [
        over_columns(tile)
        for tile in [inverse] + [exchanged(inverse, "sec", kx) for kx in range(1, sec_size)]
    ]

    results = {}
    for step in reversed(range(sec_size)):
        diagonals = diagonal(sizes, step, inverse_tiles)
        next_pieces = []
        for part in range(CHUNKS):
            partial = products(
                sizes, step, part, factor_blocks[step, part], state_pieces, factor_tiles, diagonals
            )
            total = scattered_sum(sizes, partial)
            for kx in range(sec_size):
                piece = exchanged(total, "sec", kx) if kx else total
                results[step, kx, part] = piece
                if step:
                    for kc, moved in enumerate(over_columns(piece)):
                        next_pieces.append(((kx, kc, part * chunk), moved))
        state_pieces = next_pieces

    return output(
        sizes,
        [
            results[step, kx, part]
            for step in range(sec_size)
            for kx in range(sec_size)
            for part in range(CHUNKS)
        ],
    )[None]


def solution(mesh):
    in_specs = (
        P(("groups", "sec"), "row", "col"),
        P(("groups", "sec"), "row", "col"),
        P(("groups", "row"), "col"),
    )
    out_specs = P(("groups", "sec"), "row", "col")
    return jax.shard_map(local, mesh=mesh, in_specs=in_specs, out_specs=out_specs, check_vma=False)
```

```python
import functools

import jax
import jax.numpy as jnp
from jax import lax
from jax.experimental import pallas as pl
from jax.experimental.pallas import tpu as pltpu
from jax.sharding import PartitionSpec as P

CHUNKS = 2
ANY = pl.BlockSpec(memory_space=pl.ANY)
VMEM = pl.BlockSpec(memory_space=pltpu.VMEM)
PARAMS = pltpu.CompilerParams(vmem_limit_bytes=20 * 1024 * 1024)


def exchanged(value, axis, steps):
    count = lax.axis_size(axis)
    return lax.ppermute(value, axis, [(i, (i + steps) % count) for i in range(count)])


class Sizes:
    def __init__(self, rows, cols):
        self.row = lax.axis_size("row")
        self.sec = lax.axis_size("sec")
        self.col = lax.axis_size("col")
        self.rows = rows
        self.cols = cols
        self.order = cols * self.col
        self.width = cols // self.sec
        self.chunk = self.width // CHUNKS
        self.per_tile = self.row // self.col


def chosen_copies(sizes, step, tiles, target, sems):
    sec_index, col_index = lax.axis_index("sec"), lax.axis_index("col")
    copies = []
    for kc in range(sizes.col):
        place = lax.rem(col_index - kc + sizes.col, sizes.col)
        for kx in range(sizes.sec):
            copy = pltpu.make_async_copy(tiles[kx][kc], target.at[place], sems.at[kc])
            wanted = lax.rem(sec_index - kx + sizes.sec, sizes.sec) == step
            copies.append((wanted, copy))
    return copies


def start_all(copies):
    for wanted, copy in copies:
        pl.when(wanted)(copy.start)


def wait_all(copies):
    for wanted, copy in copies:
        pl.when(wanted)(copy.wait)


def nested(refs, sizes):
    return [refs[kx * sizes.col : (kx + 1) * sizes.col] for kx in range(sizes.sec)]


def diagonal_kernel(sizes, step, *refs):
    count = sizes.sec * sizes.col
    tiles, (out, held, sems) = nested(refs[:count], sizes), refs[count:]
    copies = chosen_copies(sizes, step, tiles, held, sems)
    start_all(copies)
    wait_all(copies)
    first = lax.axis_index("sec") * sizes.width
    for k in range(CHUNKS):
        begin = pl.multiple_of(first + k * sizes.chunk, sizes.chunk)
        left = held[lax.axis_index("col"), :, pl.ds(begin, sizes.chunk)].T
        for d in range(sizes.row):
            h, i = divmod(d, sizes.per_tile)
            right = held[h, :, i * sizes.rows : (i + 1) * sizes.rows]
            out[k, d] = jnp.dot(left, right, preferred_element_type=jnp.float32)


def diagonal(sizes, step, tiles):
    flat = [tile for per_section in tiles for tile in per_section]
    shape = (CHUNKS, sizes.row, sizes.chunk, sizes.rows)
    return pl.pallas_call(
        functools.partial(diagonal_kernel, sizes, step),
        out_shape=jax.ShapeDtypeStruct(shape, jnp.float32),
        in_specs=[ANY] * len(flat),
        out_specs=VMEM,
        scratch_shapes=[
            pltpu.VMEM((sizes.col, sizes.rows, sizes.cols), jnp.bfloat16),
            pltpu.SemaphoreType.DMA((sizes.col,)),
        ],
        compiler_params=PARAMS,
        cost_estimate=pl.CostEstimate(
            flops=2 * sizes.rows * sizes.width * sizes.order,
            bytes_accessed=2 * sizes.rows * sizes.order + 4 * sizes.width * sizes.order,
            transcendentals=0,
        ),
        name="diagonal",
    )(*flat)


def panel_kernel(sizes, step, offset, own, *refs):
    *sent, out, held, sem = refs
    sec_index = lax.axis_index("sec")
    count = out.shape[0]
    begin = pl.multiple_of(sec_index * sizes.width + offset, sizes.chunk)
    copies = [(sec_index == step, pltpu.make_async_copy(own.at[:, pl.ds(begin, count)], held, sem))]
    per_section = len(sent) // (sizes.sec - 1)
    for kx in range(1, sizes.sec):
        wanted = lax.rem(sec_index - kx + sizes.sec, sizes.sec) == step
        pieces = sent[(kx - 1) * per_section : kx * per_section]
        height = count // per_section
        for k, piece in enumerate(pieces):
            target = held.at[:, k * height : (k + 1) * height]
            copies.append((wanted, pltpu.make_async_copy(piece, target, sem)))
    start_all(copies)
    wait_all(copies)
    out[...] = held[...].T


def transposed_panel(sizes, step, own, sent, part=None):
    count = sizes.width if part is None else sizes.chunk
    offset = 0 if part is None else part * sizes.chunk
    flat = [piece for pieces in sent for piece in pieces]
    return pl.pallas_call(
        functools.partial(panel_kernel, sizes, step, offset),
        out_shape=jax.ShapeDtypeStruct((count, sizes.rows), jnp.bfloat16),
        in_specs=[ANY] * (1 + len(flat)),
        out_specs=VMEM,
        scratch_shapes=[
            pltpu.VMEM((sizes.rows, count), jnp.bfloat16),
            pltpu.SemaphoreType.DMA,
        ],
        compiler_params=PARAMS,
        name="panel",
    )(own, *flat)


def products_kernel(sizes, step, part, block_rows, state_places, *refs):
    n_blocks, n_states, n_tiles = len(block_rows), len(state_places), sizes.sec * sizes.col
    blocks, refs = refs[:n_blocks], refs[n_blocks:]
    states, refs = refs[:n_states], refs[n_states:]
    tiles, refs = nested(refs[:n_tiles], sizes), refs[n_tiles:]
    diagonals, refs = refs[0], refs[1:]
    out, up_first, down_first, *refs = refs
    state, rows, added, product, tile_sems, state_sems, added_sem = refs
    row_index, sec_index, col_index = (lax.axis_index(a) for a in ("row", "sec", "col"))

    state_copies = []
    for number, (kx, kc, offset) in enumerate(state_places):
        first = lax.rem(col_index - kc + sizes.col, sizes.col) * sizes.cols + offset
        if kx is not None:
            first = first + lax.rem(sec_index - kx + sizes.sec, sizes.sec) * sizes.width
        height = states[number].shape[0]
        place = state.at[pl.ds(pl.multiple_of(first, height), height)]
        state_copies.append(pltpu.make_async_copy(states[number], place, state_sems.at[number]))
    for copy in state_copies:
        copy.start()
    tile_copies = chosen_copies(sizes, step, tiles, rows, tile_sems)
    start_all(tile_copies)
    added_copy = pltpu.make_async_copy(diagonals.at[part], added, added_sem)
    added_copy.start()
    for copy in state_copies:
        copy.wait()

    product[...] = jnp.zeros((sizes.chunk, sizes.rows), jnp.float32)

    def accumulate(ref, q):
        first = pl.multiple_of(q * sizes.rows, sizes.rows)
        count = sizes.chunk
        block = ref[...] if ref.shape[0] == count else ref[part * count : (part + 1) * count]
        product[...] += jnp.dot(
            block, state[pl.ds(first, sizes.rows)], preferred_element_type=jnp.float32
        )

    for ref, row_of in zip(blocks, block_rows):
        q, low, high = row_of(row_index)
        pl.when((q >= low) & (q <= high))(functools.partial(accumulate, ref, q))
    image = product[...].astype(jnp.bfloat16)
    wait_all(tile_copies)
    added_copy.wait()
    for d in range(sizes.row):
        h, i = divmod(d, sizes.per_tile)
        right = rows[h, :, i * sizes.rows : (i + 1) * sizes.rows]
        place = lax.rem(d - row_index + sizes.row, sizes.row)
        out[place] = jnp.dot(image, right, preferred_element_type=jnp.float32) + added[d]
    up_first[...] = out[sizes.row - 1].astype(jnp.bfloat16)
    down_first[...] = out[1].astype(jnp.bfloat16)


def products(sizes, step, part, blocks, states, tiles, diagonals):
    flat = [tile for per_section in tiles for tile in per_section]
    shape = (sizes.row, sizes.chunk, sizes.rows)
    return pl.pallas_call(
        functools.partial(
            products_kernel, sizes, step, part, [b[0] for b in blocks], [s[0] for s in states]
        ),
        out_shape=[jax.ShapeDtypeStruct(shape, jnp.float32)]
        + [jax.ShapeDtypeStruct(shape[1:], jnp.bfloat16)] * 2,
        in_specs=[VMEM] * len(blocks) + [ANY] * (len(states) + len(flat) + 1),
        out_specs=[VMEM] * 3,
        scratch_shapes=[
            pltpu.VMEM((sizes.order, sizes.rows), jnp.bfloat16),
            pltpu.VMEM((sizes.col, sizes.rows, sizes.cols), jnp.bfloat16),
            pltpu.VMEM(shape, jnp.float32),
            pltpu.VMEM(shape[1:], jnp.float32),
            pltpu.SemaphoreType.DMA((sizes.col,)),
            pltpu.SemaphoreType.DMA((len(states),)),
            pltpu.SemaphoreType.DMA,
        ],
        compiler_params=PARAMS,
        cost_estimate=pl.CostEstimate(
            flops=4 * sizes.rows * sizes.chunk * sizes.order,
            bytes_accessed=4 * sizes.rows * sizes.order + 10 * sizes.chunk * sizes.order,
            transcendentals=0,
        ),
        name="products",
    )(*[b[1] for b in blocks], *[s[1] for s in states], *flat, diagonals)


def output_kernel(sizes, *refs):
    per_step = sizes.sec * CHUNKS
    out = refs[-1]
    sec_index = lax.axis_index("sec")
    for step in range(sizes.sec):

        @pl.when(sec_index == step)
        def _():
            for kx in range(sizes.sec):
                for k in range(CHUNKS):
                    piece = refs[step * per_step + kx * CHUNKS + k][...]
                    first = lax.rem(sec_index - kx + sizes.sec, sizes.sec) * sizes.width
                    begin = pl.multiple_of(first + k * sizes.chunk, sizes.chunk)
                    out[:, pl.ds(begin, sizes.chunk)] = piece.astype(jnp.float32).T


def output(sizes, pieces):
    return pl.pallas_call(
        functools.partial(output_kernel, sizes),
        out_shape=jax.ShapeDtypeStruct((sizes.rows, sizes.cols), jnp.float32),
        in_specs=[VMEM] * len(pieces),
        out_specs=VMEM,
        compiler_params=PARAMS,
        name="output",
    )(*pieces)


def after(value, *others):
    return lax.optimization_barrier((value, *others))[0]


def neighbours_gathered(sizes, block):
    last = sizes.row - 1
    up = down = block
    found = [(lambda row: (row, 0, last), block)]
    for slot in range(last):
        up = lax.ppermute(up, "row", [(i, i + 1) for i in range(slot, last)])
        down = lax.ppermute(down, "row", [(i, i - 1) for i in range(1, sizes.row - slot)])
        found.append((lambda row, slot=slot: (row - 1 - slot, 0, last), up))
        found.append((lambda row, slot=slot: (row + 1 + slot, 0, last), down))
    return found


def trailing_gather(sizes, block):
    row_index = lax.axis_index("row")
    last = sizes.row - 1
    ups, downs = [], []
    found = [(lambda row: (row, 0, last), block)]
    for time in range(1, 2 * last):
        up = down = block
        if time > 2:
            up = jnp.where(row_index == time - 1, block, ups[-2])
            down = jnp.where(last - row_index == time - 1, block, downs[-2])
        senders = [i for i in range(last) if time // 2 <= i <= time - 1]
        ups.append(lax.ppermute(up, "row", [(i, i + 1) for i in senders]))
        downs.append(lax.ppermute(down, "row", [(last - i, last - i - 1) for i in senders]))

        def from_below(row, time=time):
            q = 2 * row - 1 - time
            return q, 0, row - 1

        def from_above(row, time=time):
            q = 2 * row - last + 1 + time
            return q, row + 1, last

        found += [(from_below, ups[-1]), (from_above, downs[-1])]
    return found


def scattered_sum(sizes, partials):
    blocks, up_first, down_first = partials
    last = sizes.row - 1
    up = down = None
    for slot in range(last):
        if slot:
            up_block = (blocks[last - slot] + up.astype(jnp.float32)).astype(jnp.bfloat16)
            down_block = (blocks[slot + 1] + down.astype(jnp.float32)).astype(jnp.bfloat16)
        else:
            up_block, down_block = up_first, down_first
        up = lax.ppermute(up_block, "row", [(i, i + 1) for i in range(slot + 1)])
        down = lax.ppermute(
            down_block, "row", [(i, i - 1) for i in range(last - slot, last + 1)]
        )
    total = blocks[0] + up.astype(jnp.float32) + down.astype(jnp.float32)
    return total.astype(jnp.bfloat16)


def local(factors, inverses, sigma_end):
    step_count, rows, cols = factors.shape
    assert step_count == 1
    sizes = Sizes(rows, cols)
    sec_size, col_size, width, chunk = sizes.sec, sizes.col, sizes.width, sizes.chunk
    sec_index = lax.axis_index("sec")

    def panel(tile, offset, part=None):
        first = (sec_index + offset) % sec_size * width
        if part is None:
            return lax.dynamic_slice_in_dim(tile, first, width, 1)
        return lax.dynamic_slice_in_dim(tile, first + part * chunk, chunk, 1)

    factor, inverse = factors[0], inverses[0]

    arrived_chunks = [None]
    for kx in range(1, sec_size):
        arrived_chunks.append(
            [exchanged(panel(factor, kx, part), "sec", kx) for part in range(CHUNKS)]
        )

    factor_blocks = {}
    last = sec_size - 1
    for part in range(CHUNKS):
        sent = [[chunks[part]] for chunks in arrived_chunks[1:]]
        block = transposed_panel(sizes, last, factor, sent, part)
        factor_blocks[last, part] = neighbours_gathered(sizes, block)
    for step in reversed(range(last)):
        block = transposed_panel(sizes, step, factor, arrived_chunks[1:])
        block = after(block, *[array for _, array in factor_blocks[step + 1, CHUNKS - 1][:3]])
        blocks = trailing_gather(sizes, block)
        for part in range(CHUNKS):
            factor_blocks[step, part] = blocks

    swapped = [chunks[-1] for chunks in arrived_chunks[1:]]

    def tiles_over_sections(tile, first_chunks):
        found = [tile]
        for kx in range(1, sec_size):
            whole = jnp.zeros_like(tile)
            for j in range(sec_size):
                if j == 0 and first_chunks is not None:
                    piece = jnp.concatenate(first_chunks[kx], axis=1)
                else:
                    piece = exchanged(after(panel(tile, kx + j), *swapped), "sec", kx)
                first = (sec_index + j) % sec_size * width
                whole = lax.dynamic_update_slice_in_dim(whole, piece, first, 1)
            found.append(whole)
        return found

    def over_columns(value):
        return [value] + [exchanged(value, "col", kc) for kc in range(1, col_size)]

    state_pieces = [
        ((None, kc, 0), piece)
        for kc, piece in enumerate(over_columns(sigma_end.astype(jnp.bfloat16).T))
    ]
    factor_tiles = [over_columns(tile) for tile in tiles_over_sections(factor, arrived_chunks)]
    inverse_tiles = [
        over_columns(tile)
        for tile in [inverse]
        + [exchanged(after(inverse, *swapped), "sec", kx) for kx in range(1, sec_size)]
    ]

    results = {}
    for step in reversed(range(sec_size)):
        diagonals = diagonal(sizes, step, inverse_tiles)
        next_pieces = []
        for part in range(CHUNKS):
            partial = products(
                sizes, step, part, factor_blocks[step, part], state_pieces, factor_tiles, diagonals
            )
            total = scattered_sum(sizes, partial)
            for kx in range(sec_size):
                piece = exchanged(total, "sec", kx) if kx else total
                results[step, kx, part] = piece
                if step:
                    for kc, moved in enumerate(over_columns(piece)):
                        next_pieces.append(((kx, kc, part * chunk), moved))
        state_pieces = next_pieces

    return output(
        sizes,
        [
            results[step, kx, part]
            for step in range(sec_size)
            for kx in range(sec_size)
            for part in range(CHUNKS)
        ],
    )[None]


def solution(mesh):
    in_specs = (
        P(("groups", "sec"), "row", "col"),
        P(("groups", "sec"), "row", "col"),
        P(("groups", "row"), "col"),
    )
    out_specs = P(("groups", "sec"), "row", "col")
    return jax.shard_map(local, mesh=mesh, in_specs=in_specs, out_specs=out_specs, check_vma=False)
```

```python
import functools

import jax
import jax.numpy as jnp
from jax import lax
from jax.experimental import pallas as pl
from jax.experimental.pallas import tpu as pltpu
from jax.sharding import PartitionSpec as P

CHUNKS = 2
ANY = pl.BlockSpec(memory_space=pl.ANY)
VMEM = pl.BlockSpec(memory_space=pltpu.VMEM)
PARAMS = pltpu.CompilerParams(vmem_limit_bytes=16 * 1024 * 1024)


def exchanged(value, axis, steps):
    count = lax.axis_size(axis)
    return lax.ppermute(value, axis, [(i, (i + steps) % count) for i in range(count)])


class Sizes:
    def __init__(self, rows, cols):
        self.row = lax.axis_size("row")
        self.sec = lax.axis_size("sec")
        self.col = lax.axis_size("col")
        self.rows = rows
        self.cols = cols
        self.order = cols * self.col
        self.width = cols // self.sec
        self.chunk = self.width // CHUNKS
        self.per_tile = self.row // self.col


def chosen_copies(sizes, step, tiles, target, sems):
    sec_index, col_index = lax.axis_index("sec"), lax.axis_index("col")
    copies = []
    for kc in range(sizes.col):
        place = lax.rem(col_index - kc + sizes.col, sizes.col)
        for kx in range(sizes.sec):
            copy = pltpu.make_async_copy(tiles[kx][kc], target.at[place], sems.at[kc])
            wanted = lax.rem(sec_index - kx + sizes.sec, sizes.sec) == step
            copies.append((wanted, copy))
    return copies


def start_all(copies):
    for wanted, copy in copies:
        pl.when(wanted)(copy.start)


def wait_all(copies):
    for wanted, copy in copies:
        pl.when(wanted)(copy.wait)


def nested(refs, sizes):
    return [refs[kx * sizes.col : (kx + 1) * sizes.col] for kx in range(sizes.sec)]


def panel_kernel(sizes, step, offset, own, *refs):
    *sent, out, held, sem = refs
    sec_index = lax.axis_index("sec")
    count = out.shape[0]
    begin = pl.multiple_of(sec_index * sizes.width + offset, sizes.chunk)
    copies = [(sec_index == step, pltpu.make_async_copy(own.at[:, pl.ds(begin, count)], held, sem))]
    per_section = len(sent) // (sizes.sec - 1)
    for kx in range(1, sizes.sec):
        wanted = lax.rem(sec_index - kx + sizes.sec, sizes.sec) == step
        pieces = sent[(kx - 1) * per_section : kx * per_section]
        height = count // per_section
        for k, piece in enumerate(pieces):
            target = held.at[:, k * height : (k + 1) * height]
            copies.append((wanted, pltpu.make_async_copy(piece, target, sem)))
    start_all(copies)
    wait_all(copies)
    out[...] = held[...].T


def transposed_panel(sizes, step, own, sent, part=None):
    count = sizes.width if part is None else sizes.chunk
    offset = 0 if part is None else part * sizes.chunk
    flat = [piece for pieces in sent for piece in pieces]
    return pl.pallas_call(
        functools.partial(panel_kernel, sizes, step, offset),
        out_shape=jax.ShapeDtypeStruct((count, sizes.rows), jnp.bfloat16),
        in_specs=[ANY] * (1 + len(flat)),
        out_specs=VMEM,
        scratch_shapes=[
            pltpu.VMEM((sizes.rows, count), jnp.bfloat16),
            pltpu.SemaphoreType.DMA,
        ],
        compiler_params=PARAMS,
        name="panel",
    )(own, *flat)


def products_kernel(sizes, step, part, block_rows, state_places, *refs):
    n_blocks, n_states, n_tiles = len(block_rows), len(state_places), sizes.sec * sizes.col
    blocks, refs = refs[:n_blocks], refs[n_blocks:]
    states, refs = refs[:n_states], refs[n_states:]
    tiles, refs = nested(refs[:n_tiles], sizes), refs[n_tiles:]
    inverse_tiles, refs = nested(refs[:n_tiles], sizes), refs[n_tiles:]
    out, up_first, down_first, *refs = refs
    state, rows, inverses, product, tile_sems, inverse_sems, state_sems = refs
    row_index, sec_index, col_index = (lax.axis_index(a) for a in ("row", "sec", "col"))

    state_copies = []
    for number, (kx, kc, offset) in enumerate(state_places):
        first = lax.rem(col_index - kc + sizes.col, sizes.col) * sizes.cols + offset
        if kx is not None:
            first = first + lax.rem(sec_index - kx + sizes.sec, sizes.sec) * sizes.width
        height = states[number].shape[0]
        place = state.at[pl.ds(pl.multiple_of(first, height), height)]
        state_copies.append(pltpu.make_async_copy(states[number], place, state_sems.at[number]))
    for copy in state_copies:
        copy.start()
    tile_copies = chosen_copies(sizes, step, tiles, rows, tile_sems)
    start_all(tile_copies)
    inverse_copies = chosen_copies(sizes, step, inverse_tiles, inverses, inverse_sems)
    start_all(inverse_copies)
    for copy in state_copies:
        copy.wait()

    product[...] = jnp.zeros((sizes.chunk, sizes.rows), jnp.float32)

    def accumulate(ref, q):
        first = pl.multiple_of(q * sizes.rows, sizes.rows)
        count = sizes.chunk
        block = ref[...] if ref.shape[0] == count else ref[part * count : (part + 1) * count]
        product[...] += jnp.dot(
            block, state[pl.ds(first, sizes.rows)], preferred_element_type=jnp.float32
        )

    for ref, row_of in zip(blocks, block_rows):
        q, low, high = row_of(row_index)
        pl.when((q >= low) & (q <= high))(functools.partial(accumulate, ref, q))
    image = product[...].astype(jnp.bfloat16)
    wait_all(tile_copies)
    wait_all(inverse_copies)
    begin = pl.multiple_of(sec_index * sizes.width + part * sizes.chunk, sizes.chunk)
    left = inverses[col_index, :, pl.ds(begin, sizes.chunk)].T
    for d in range(sizes.row):
        h, i = divmod(d, sizes.per_tile)
        block = slice(i * sizes.rows, (i + 1) * sizes.rows)
        place = lax.rem(d - row_index + sizes.row, sizes.row)
        out[place] = jnp.dot(
            image, rows[h, :, block], preferred_element_type=jnp.float32
        ) + jnp.dot(left, inverses[h, :, block], preferred_element_type=jnp.float32)
    up_first[...] = out[sizes.row - 1].astype(jnp.bfloat16)
    down_first[...] = out[1].astype(jnp.bfloat16)


def products(sizes, step, part, blocks, states, tiles, inverse_tiles):
    flat = [tile for per_section in tiles + inverse_tiles for tile in per_section]
    shape = (sizes.row, sizes.chunk, sizes.rows)
    return pl.pallas_call(
        functools.partial(
            products_kernel, sizes, step, part, [b[0] for b in blocks], [s[0] for s in states]
        ),
        out_shape=[jax.ShapeDtypeStruct(shape, jnp.float32)]
        + [jax.ShapeDtypeStruct(shape[1:], jnp.bfloat16)] * 2,
        in_specs=[VMEM] * len(blocks) + [ANY] * (len(states) + len(flat)),
        out_specs=[VMEM] * 3,
        scratch_shapes=[
            pltpu.VMEM((sizes.order, sizes.rows), jnp.bfloat16),
            pltpu.VMEM((sizes.col, sizes.rows, sizes.cols), jnp.bfloat16),
            pltpu.VMEM((sizes.col, sizes.rows, sizes.cols), jnp.bfloat16),
            pltpu.VMEM(shape[1:], jnp.float32),
            pltpu.SemaphoreType.DMA((sizes.col,)),
            pltpu.SemaphoreType.DMA((sizes.col,)),
            pltpu.SemaphoreType.DMA((len(states),)),
        ],
        compiler_params=PARAMS,
        cost_estimate=pl.CostEstimate(
            flops=6 * sizes.rows * sizes.chunk * sizes.order,
            bytes_accessed=4 * sizes.rows * sizes.order + 10 * sizes.chunk * sizes.order,
            transcendentals=0,
        ),
        name="products",
    )(*[b[1] for b in blocks], *[s[1] for s in states], *flat)


def output_kernel(sizes, *refs):
    per_step = sizes.sec * CHUNKS
    out = refs[-1]
    sec_index = lax.axis_index("sec")
    for step in range(sizes.sec):

        @pl.when(sec_index == step)
        def _():
            for kx in range(sizes.sec):
                for k in range(CHUNKS):
                    piece = refs[step * per_step + kx * CHUNKS + k][...]
                    first = lax.rem(sec_index - kx + sizes.sec, sizes.sec) * sizes.width
                    begin = pl.multiple_of(first + k * sizes.chunk, sizes.chunk)
                    out[:, pl.ds(begin, sizes.chunk)] = piece.astype(jnp.float32).T


def output(sizes, pieces):
    return pl.pallas_call(
        functools.partial(output_kernel, sizes),
        out_shape=jax.ShapeDtypeStruct((sizes.rows, sizes.cols), jnp.float32),
        in_specs=[VMEM] * len(pieces),
        out_specs=VMEM,
        compiler_params=PARAMS,
        name="output",
    )(*pieces)


def after(value, *others):
    return lax.optimization_barrier((value, *others))[0]


def neighbours_gathered(sizes, block):
    last = sizes.row - 1
    up = down = block
    found = [(lambda row: (row, 0, last), block)]
    for slot in range(last):
        up = lax.ppermute(up, "row", [(i, i + 1) for i in range(slot, last)])
        down = lax.ppermute(down, "row", [(i, i - 1) for i in range(1, sizes.row - slot)])
        found.append((lambda row, slot=slot: (row - 1 - slot, 0, last), up))
        found.append((lambda row, slot=slot: (row + 1 + slot, 0, last), down))
    return found


def first_slot(sizes, block):
    last = sizes.row - 1
    up = lax.ppermute(block, "row", [(i, i + 1) for i in range(last)])
    down = lax.ppermute(block, "row", [(i, i - 1) for i in range(1, sizes.row)])
    return up, down


def scattered_sum(sizes, partials, gather=None):
    blocks, up_first, down_first = partials
    row_index = lax.axis_index("row")
    last = sizes.row - 1
    up = down = None
    found = []
    for slot in range(last):
        if slot:
            up_block = (blocks[last - slot] + up.astype(jnp.float32)).astype(jnp.bfloat16)
            down_block = (blocks[slot + 1] + down.astype(jnp.float32)).astype(jnp.bfloat16)
        else:
            up_block, down_block = up_first, down_first
        low = slot
        if gather is not None:
            if slot == 0:
                up, down = gather
            if slot < last - 1:
                up_block = jnp.where(row_index <= slot, up_block, up)
                down_block = jnp.where(last - row_index <= slot, down_block, down)
                low = last - 1
        up = lax.ppermute(up_block, "row", [(i, i + 1) for i in range(low + 1)])
        down = lax.ppermute(
            down_block, "row", [(i, i - 1) for i in range(last - low, last + 1)]
        )
        if gather is not None and slot < last - 1:
            found.append((lambda row, slot=slot: (row - 2 - slot, 0, last), up))
            found.append((lambda row, slot=slot: (row + 2 + slot, 0, last), down))
    total = blocks[0] + up.astype(jnp.float32) + down.astype(jnp.float32)
    return total.astype(jnp.bfloat16), found


def local(factors, inverses, sigma_end):
    step_count, rows, cols = factors.shape
    assert step_count == 1
    sizes = Sizes(rows, cols)
    sec_size, col_size, width, chunk = sizes.sec, sizes.col, sizes.width, sizes.chunk
    sec_index = lax.axis_index("sec")

    def panel(tile, offset, part=None):
        first = (sec_index + offset) % sec_size * width
        if part is None:
            return lax.dynamic_slice_in_dim(tile, first, width, 1)
        return lax.dynamic_slice_in_dim(tile, first + part * chunk, chunk, 1)

    factor, inverse = factors[0], inverses[0]

    arrived_chunks = [None]
    for kx in range(1, sec_size):
        arrived_chunks.append(
            [exchanged(panel(factor, kx, part), "sec", kx) for part in range(CHUNKS)]
        )

    factor_blocks = {}
    last = sec_size - 1
    for part in range(CHUNKS):
        sent = [[chunks[part]] for chunks in arrived_chunks[1:]]
        block = transposed_panel(sizes, last, factor, sent, part)
        factor_blocks[last, part] = neighbours_gathered(sizes, block)
    swapped = [chunk for chunks in arrived_chunks[1:] for chunk in chunks]

    def tiles_over_sections(tile, first_chunks):
        found = [tile]
        for kx in range(1, sec_size):
            whole = jnp.zeros_like(tile)
            for j in range(sec_size):
                if j == 0 and first_chunks is not None:
                    piece = jnp.concatenate(first_chunks[kx], axis=1)
                else:
                    piece = exchanged(after(panel(tile, kx + j), *swapped), "sec", kx)
                first = (sec_index + j) % sec_size * width
                whole = lax.dynamic_update_slice_in_dim(whole, piece, first, 1)
            found.append(whole)
        return found

    def over_columns(value):
        return [value] + [exchanged(value, "col", kc) for kc in range(1, col_size)]

    state_pieces = [
        ((None, kc, 0), piece)
        for kc, piece in enumerate(over_columns(sigma_end.astype(jnp.bfloat16).T))
    ]
    factor_tiles = [over_columns(tile) for tile in tiles_over_sections(factor, arrived_chunks)]
    inverse_tiles = [
        over_columns(tile)
        for tile in [inverse]
        + [exchanged(after(inverse, *swapped), "sec", kx) for kx in range(1, sec_size)]
    ]

    results = {}
    for step in reversed(range(sec_size)):
        trailing = []
        if step:
            earlier = [array for k in range(CHUNKS) for _, array in factor_blocks[step, k][-2:]]
            for part in range(CHUNKS):
                sent = [[chunks[part]] for chunks in arrived_chunks[1:]]
                block = after(transposed_panel(sizes, step - 1, factor, sent, part), *earlier)
                trailing.append((block, first_slot(sizes, block)))
        next_pieces = []
        for part in range(CHUNKS):
            partials = products(
                sizes, step, part, factor_blocks[step, part], state_pieces, factor_tiles, inverse_tiles
            )
            if step:
                block, (up, down) = trailing[part]
                total, found = scattered_sum(sizes, partials, (up, down))
                edge = sizes.row - 1
                factor_blocks[step - 1, part] = [
                    (lambda row: (row, 0, edge), block),
                    (lambda row: (row - 1, 0, edge), up),
                    (lambda row: (row + 1, 0, edge), down),
                    *found,
                ]
            else:
                total, _ = scattered_sum(sizes, partials)
            for kx in range(sec_size):
                piece = exchanged(total, "sec", kx) if kx else total
                results[step, kx, part] = piece
                if step:
                    for kc, moved in enumerate(over_columns(piece)):
                        next_pieces.append(((kx, kc, part * chunk), moved))
        state_pieces = next_pieces

    return output(
        sizes,
        [
            results[step, kx, part]
            for step in range(sec_size)
            for kx in range(sec_size)
            for part in range(CHUNKS)
        ],
    )[None]


def solution(mesh):
    in_specs = (
        P(("groups", "sec"), "row", "col"),
        P(("groups", "sec"), "row", "col"),
        P(("groups", "row"), "col"),
    )
    out_specs = P(("groups", "sec"), "row", "col")
    return jax.shard_map(local, mesh=mesh, in_specs=in_specs, out_specs=out_specs, check_vma=False)
```

```python
import functools

import jax
import jax.numpy as jnp
from jax import lax
from jax.experimental import pallas as pl
from jax.experimental.pallas import tpu as pltpu
from jax.sharding import PartitionSpec as P

CHUNKS = 2
ANY = pl.BlockSpec(memory_space=pl.ANY)
VMEM = pl.BlockSpec(memory_space=pltpu.VMEM)
PARAMS = pltpu.CompilerParams(vmem_limit_bytes=16 * 1024 * 1024)


def exchanged(value, axis, steps):
    count = lax.axis_size(axis)
    return lax.ppermute(value, axis, [(i, (i + steps) % count) for i in range(count)])


class Sizes:
    def __init__(self, rows, cols):
        self.row = lax.axis_size("row")
        self.sec = lax.axis_size("sec")
        self.col = lax.axis_size("col")
        self.rows = rows
        self.cols = cols
        self.order = cols * self.col
        self.width = cols // self.sec
        self.chunk = self.width // CHUNKS
        self.per_tile = self.row // self.col


def chosen_copies(sizes, step, tiles, target, top, sems):
    sec_index, col_index = lax.axis_index("sec"), lax.axis_index("col")
    copies = []
    for kc in range(sizes.col):
        begin = lax.rem(col_index - kc + sizes.col, sizes.col) * sizes.cols
        place = target.at[top : top + sizes.rows, pl.ds(pl.multiple_of(begin, sizes.cols), sizes.cols)]
        for kx in range(sizes.sec):
            copy = pltpu.make_async_copy(tiles[kx][kc], place, sems.at[kc])
            wanted = lax.rem(sec_index - kx + sizes.sec, sizes.sec) == step
            copies.append((wanted, copy))
    return copies


def start_all(copies):
    for wanted, copy in copies:
        copy.start() if wanted is True else pl.when(wanted)(copy.start)


def wait_all(copies):
    for wanted, copy in copies:
        copy.wait() if wanted is True else pl.when(wanted)(copy.wait)


def nested(refs, sizes):
    return [refs[kx * sizes.col : (kx + 1) * sizes.col] for kx in range(sizes.sec)]


def panel_kernel(sizes, step, offset, own, *refs):
    *sent, out, held, sem = refs
    sec_index = lax.axis_index("sec")
    count = out.shape[0]
    begin = pl.multiple_of(sec_index * sizes.width + offset, sizes.chunk)
    copies = [(sec_index == step, pltpu.make_async_copy(own.at[:, pl.ds(begin, count)], held, sem))]
    per_section = len(sent) // (sizes.sec - 1)
    for kx in range(1, sizes.sec):
        wanted = lax.rem(sec_index - kx + sizes.sec, sizes.sec) == step
        pieces = sent[(kx - 1) * per_section : kx * per_section]
        height = count // per_section
        for k, piece in enumerate(pieces):
            target = held.at[:, k * height : (k + 1) * height]
            copies.append((wanted, pltpu.make_async_copy(piece, target, sem)))
    start_all(copies)
    wait_all(copies)
    out[...] = held[...].T


def transposed_panel(sizes, step, own, sent, part=None):
    count = sizes.width if part is None else sizes.chunk
    offset = 0 if part is None else part * sizes.chunk
    flat = [piece for pieces in sent for piece in pieces]
    return pl.pallas_call(
        functools.partial(panel_kernel, sizes, step, offset),
        out_shape=jax.ShapeDtypeStruct((count, sizes.rows), jnp.bfloat16),
        in_specs=[ANY] * (1 + len(flat)),
        out_specs=VMEM,
        scratch_shapes=[
            pltpu.VMEM((sizes.rows, count), jnp.bfloat16),
            pltpu.SemaphoreType.DMA,
        ],
        compiler_params=PARAMS,
        name="panel",
    )(own, *flat)


def products_kernel(sizes, step, part, block_rows, state_places, *refs):
    n_blocks, n_states, n_tiles = len(block_rows), len(state_places), sizes.sec * sizes.col
    blocks, refs = refs[:n_blocks], refs[n_blocks:]
    states, refs = refs[:n_states], refs[n_states:]
    tiles, refs = nested(refs[:n_tiles], sizes), refs[n_tiles:]
    inverse_tiles, refs = nested(refs[:n_tiles], sizes), refs[n_tiles:]
    out, up_first, down_first, *refs = refs
    panel, state, rows, left, block_sems, state_sems, tile_sems = refs
    row_index, sec_index, col_index = (lax.axis_index(a) for a in ("row", "sec", "col"))
    count = sizes.chunk

    first_copies = []
    for number, (kx, kc, offset) in enumerate(state_places):
        first = lax.rem(col_index - kc + sizes.col, sizes.col) * sizes.cols + offset
        if kx is not None:
            first = first + lax.rem(sec_index - kx + sizes.sec, sizes.sec) * sizes.width
        height = states[number].shape[0]
        place = state.at[pl.ds(pl.multiple_of(first, height), height)]
        copy = pltpu.make_async_copy(states[number], place, state_sems.at[number])
        first_copies.append((True, copy))
    for number, (ref, row_of) in enumerate(zip(blocks, block_rows)):
        q, low, high = row_of(row_index)
        wanted = (q >= low) & (q <= high)
        source = ref if ref.shape[0] == count else ref.at[part * count : (part + 1) * count]
        begin = pl.multiple_of(jnp.clip(q, 0, sizes.row - 1) * sizes.rows, sizes.rows)
        place = panel.at[:, pl.ds(begin, sizes.rows)]
        first_copies.append((wanted, pltpu.make_async_copy(source, place, block_sems.at[number])))
    start_all(first_copies)
    tile_copies = []
    for number, array in enumerate((tiles, inverse_tiles)):
        tile_copies += chosen_copies(sizes, step, array, rows, number * sizes.rows, tile_sems.at[number])
    start_all(tile_copies)

    wait_all(first_copies)
    image = jnp.dot(panel[...], state[...], preferred_element_type=jnp.float32)
    left[:, : sizes.rows] = image.astype(jnp.bfloat16)
    wait_all(tile_copies)
    begin = col_index * sizes.cols + sec_index * sizes.width + part * count
    inverse_panel = rows[sizes.rows :, pl.ds(pl.multiple_of(begin, count), count)]
    left[:, sizes.rows :] = inverse_panel.T
    for d in range(sizes.row):
        place = lax.rem(d - row_index + sizes.row, sizes.row)
        out[place] = jnp.dot(
            left[...],
            rows[:, d * sizes.rows : (d + 1) * sizes.rows],
            preferred_element_type=jnp.float32,
        )
    up_first[...] = out[sizes.row - 1].astype(jnp.bfloat16)
    down_first[...] = out[1].astype(jnp.bfloat16)


def products(sizes, step, part, blocks, states, tiles, inverse_tiles):
    flat = [tile for per_section in tiles + inverse_tiles for tile in per_section]
    shape = (sizes.row, sizes.chunk, sizes.rows)
    return pl.pallas_call(
        functools.partial(
            products_kernel, sizes, step, part, [b[0] for b in blocks], [s[0] for s in states]
        ),
        out_shape=[jax.ShapeDtypeStruct(shape, jnp.float32)]
        + [jax.ShapeDtypeStruct(shape[1:], jnp.bfloat16)] * 2,
        in_specs=[ANY] * (len(blocks) + len(states) + len(flat)),
        out_specs=[VMEM] * 3,
        scratch_shapes=[
            pltpu.VMEM((sizes.chunk, sizes.order), jnp.bfloat16),
            pltpu.VMEM((sizes.order, sizes.rows), jnp.bfloat16),
            pltpu.VMEM((2 * sizes.rows, sizes.order), jnp.bfloat16),
            pltpu.VMEM((sizes.chunk, 2 * sizes.rows), jnp.bfloat16),
            pltpu.SemaphoreType.DMA((len(blocks),)),
            pltpu.SemaphoreType.DMA((len(states),)),
            pltpu.SemaphoreType.DMA((2, sizes.col)),
        ],
        compiler_params=PARAMS,
        cost_estimate=pl.CostEstimate(
            flops=6 * sizes.rows * sizes.chunk * sizes.order,
            bytes_accessed=6 * sizes.rows * sizes.order + 6 * sizes.chunk * sizes.order,
            transcendentals=0,
        ),
        name="products",
    )(*[b[1] for b in blocks], *[s[1] for s in states], *flat)


def output_kernel(sizes, *refs):
    per_step = sizes.sec * CHUNKS
    out = refs[-1]
    sec_index = lax.axis_index("sec")
    for step in range(sizes.sec):

        @pl.when(sec_index == step)
        def _():
            for kx in range(sizes.sec):
                for k in range(CHUNKS):
                    piece = refs[step * per_step + kx * CHUNKS + k][...]
                    first = lax.rem(sec_index - kx + sizes.sec, sizes.sec) * sizes.width
                    begin = pl.multiple_of(first + k * sizes.chunk, sizes.chunk)
                    out[:, pl.ds(begin, sizes.chunk)] = piece.astype(jnp.float32).T


def output(sizes, pieces):
    return pl.pallas_call(
        functools.partial(output_kernel, sizes),
        out_shape=jax.ShapeDtypeStruct((sizes.rows, sizes.cols), jnp.float32),
        in_specs=[VMEM] * len(pieces),
        out_specs=VMEM,
        compiler_params=PARAMS,
        name="output",
    )(*pieces)


def after(value, *others):
    return lax.optimization_barrier((value, *others))[0]


def neighbours_gathered(sizes, block):
    last = sizes.row - 1
    up = down = block
    found = [(lambda row: (row, 0, last), block)]
    for slot in range(last):
        up = lax.ppermute(up, "row", [(i, i + 1) for i in range(slot, last)])
        down = lax.ppermute(down, "row", [(i, i - 1) for i in range(1, sizes.row - slot)])
        found.append((lambda row, slot=slot: (row - 1 - slot, 0, last), up))
        found.append((lambda row, slot=slot: (row + 1 + slot, 0, last), down))
    return found


class TrailingGather:
    def __init__(self, sizes, panel):
        self.sizes = sizes
        self.panel = panel
        self.last = sizes.row - 1
        row_index = lax.axis_index("row")
        self.places = (row_index, self.last - row_index)
        self.got = {}

    def own(self, part):
        if part is None:
            return self.panel
        return self.panel[part * self.sizes.chunk : (part + 1) * self.sizes.chunk]

    def received(self, time, part, way):
        if (time, None) in self.got:
            array = self.got[time, None][way]
            if part is None:
                return array
            return array[part * self.sizes.chunk : (part + 1) * self.sizes.chunk]
        return self.got[time, part][way]

    def payload(self, time, part, way):
        if time <= 2:
            return self.own(part)
        earlier = self.received(time - 2, part, way)
        if time > self.last:
            return earlier
        return jnp.where(self.places[way] == time - 1, self.own(part), earlier)

    def send(self, time, part, others=()):
        senders = range(time // 2, min(time, self.last))
        self.got[time, part] = [
            lax.ppermute(
                after(self.payload(time, part, way), *others), "row", pairs(self.sizes, senders, way)
            )
            for way in range(2)
        ]

    def blocks(self, part):
        last = self.last
        found = [(lambda row: (row, 0, last), self.panel)]
        for (time, piece), (up, down) in self.got.items():
            if piece in (None, part):
                found.append((lambda row, time=time: (2 * row - 1 - time, 0, row - 1), up))
                found.append((lambda row, time=time: (2 * row - last + 1 + time, row + 1, last), down))
        return found


def pairs(sizes, senders, way):
    last = sizes.row - 1
    return [(last - i, last - i - 1) if way else (i, i + 1) for i in senders]


def scattered_sum(sizes, partials, part, gather=None):
    blocks, *first = partials
    row_index = lax.axis_index("row")
    last = sizes.row - 1
    places = (row_index, last - row_index)
    arrived = None
    for slot in range(last):
        passed = []
        riding = gather is not None and slot < last - 1
        for way in range(2):
            block = first[way]
            if slot:
                own = blocks[slot + 1 if way else last - slot]
                block = (own + arrived[way].astype(jnp.float32)).astype(jnp.bfloat16)
            senders = range(slot + 1)
            if riding:
                block = jnp.where(
                    places[way] <= slot, block, gather.payload(last + slot, part, way)
                )
                senders = range(last)
            passed.append(lax.ppermute(block, "row", pairs(sizes, senders, way)))
        arrived = passed
        if riding:
            gather.got[last + slot, part] = passed
    total = blocks[0] + arrived[0].astype(jnp.float32) + arrived[1].astype(jnp.float32)
    return total.astype(jnp.bfloat16)


def local(factors, inverses, sigma_end):
    step_count, rows, cols = factors.shape
    assert step_count == 1
    sizes = Sizes(rows, cols)
    sec_size, col_size, width, chunk = sizes.sec, sizes.col, sizes.width, sizes.chunk
    sec_index = lax.axis_index("sec")

    def panel(tile, offset, part=None):
        first = (sec_index + offset) % sec_size * width
        if part is None:
            return lax.dynamic_slice_in_dim(tile, first, width, 1)
        return lax.dynamic_slice_in_dim(tile, first + part * chunk, chunk, 1)

    factor, inverse = factors[0], inverses[0]

    arrived_chunks = [[] for _ in range(sec_size)]
    for part in range(CHUNKS):
        earlier = [chunks[-1] for chunks in arrived_chunks[1:] if chunks]
        for kx in range(1, sec_size):
            piece = after(panel(factor, kx, part), *earlier)
            arrived_chunks[kx].append(exchanged(piece, "sec", kx))

    factor_blocks = {}
    last = sec_size - 1
    for part in range(CHUNKS):
        sent = [[chunks[part]] for chunks in arrived_chunks[1:]]
        block = transposed_panel(sizes, last, factor, sent, part)
        factor_blocks[last, part] = neighbours_gathered(sizes, block)
    swapped = [chunk for chunks in arrived_chunks[1:] for chunk in chunks]

    def tiles_over_sections(tile, first_chunks):
        found = [tile]
        for kx in range(1, sec_size):
            whole = jnp.zeros_like(tile)
            for j in range(sec_size):
                if j == 0 and first_chunks is not None:
                    piece = jnp.concatenate(first_chunks[kx], axis=1)
                else:
                    piece = exchanged(after(panel(tile, kx + j), *swapped), "sec", kx)
                first = (sec_index + j) % sec_size * width
                whole = lax.dynamic_update_slice_in_dim(whole, piece, first, 1)
            found.append(whole)
        return found

    def over_columns(value):
        return [value] + [exchanged(value, "col", kc) for kc in range(1, col_size)]

    state_pieces = [
        ((None, kc, 0), piece)
        for kc, piece in enumerate(over_columns(sigma_end.astype(jnp.bfloat16).T))
    ]
    factor_tiles = [over_columns(tile) for tile in tiles_over_sections(factor, arrived_chunks)]
    inverse_tiles = [
        over_columns(tile)
        for tile in [inverse]
        + [exchanged(after(inverse, *swapped), "sec", kx) for kx in range(1, sec_size)]
    ]

    results = {}
    for step in reversed(range(sec_size)):
        gather = None
        if step:
            gather = TrailingGather(
                sizes, transposed_panel(sizes, step - 1, factor, arrived_chunks[1:])
            )
            for time in range(1, sizes.row - 1):
                others = []
                if step == last:
                    others = [a for _, a in factor_blocks[step, CHUNKS - 1][2 * time - 1 : 2 * time + 1]]
                gather.send(time, None, others)
        next_pieces = []
        for part in range(CHUNKS):
            partials = products(
                sizes, step, part, factor_blocks[step, part], state_pieces, factor_tiles, inverse_tiles
            )
            total = scattered_sum(sizes, partials, part, gather)
            if step:
                gather.send(2 * sizes.row - 3, part, [total])
                factor_blocks[step - 1, part] = gather.blocks(part)
            for kx in range(sec_size):
                piece = exchanged(total, "sec", kx) if kx else total
                results[step, kx, part] = piece
                if step:
                    for kc, moved in enumerate(over_columns(piece)):
                        next_pieces.append(((kx, kc, part * chunk), moved))
        state_pieces = next_pieces

    return output(
        sizes,
        [
            results[step, kx, part]
            for step in range(sec_size)
            for kx in range(sec_size)
            for part in range(CHUNKS)
        ],
    )[None]


def solution(mesh):
    in_specs = (
        P(("groups", "sec"), "row", "col"),
        P(("groups", "sec"), "row", "col"),
        P(("groups", "row"), "col"),
    )
    out_specs = P(("groups", "sec"), "row", "col")
    return jax.shard_map(local, mesh=mesh, in_specs=in_specs, out_specs=out_specs, check_vma=False)
```

```python
import functools

import jax
import jax.numpy as jnp
from jax import lax
from jax.experimental import pallas as pl
from jax.experimental.pallas import tpu as pltpu
from jax.sharding import PartitionSpec as P

CHUNKS = 2
HBM = pl.BlockSpec(memory_space=pltpu.HBM)
VMEM = pl.BlockSpec(memory_space=pltpu.VMEM)
PARAMS = pltpu.CompilerParams(vmem_limit_bytes=16 * 1024 * 1024)


def exchanged(value, axis, steps):
    count = lax.axis_size(axis)
    return lax.ppermute(value, axis, [(i, (i + steps) % count) for i in range(count)])


class Sizes:
    def __init__(self, rows, cols):
        self.row = lax.axis_size("row")
        self.sec = lax.axis_size("sec")
        self.col = lax.axis_size("col")
        self.rows = rows
        self.cols = cols
        self.order = cols * self.col
        self.width = cols // self.sec
        self.chunk = self.width // CHUNKS
        self.per_tile = self.row // self.col


def chosen_copies(sizes, step, tiles, target, top, sems):
    sec_index, col_index = lax.axis_index("sec"), lax.axis_index("col")
    copies = []
    for kx in range(sizes.sec):
        wanted = lax.rem(sec_index - kx + sizes.sec, sizes.sec) == step
        for kc in range(sizes.col):
            tile = lax.rem(col_index - kc + sizes.col, sizes.col) * sizes.cols
            for number, (array, source, panel, offset) in enumerate(tiles[kx][kc]):
                begin = tile + offset
                if panel is not None:
                    begin = begin + lax.rem(sec_index + panel, sizes.sec) * sizes.width
                first, count = source
                place = target.at[
                    top : top + sizes.rows, pl.ds(pl.multiple_of(begin, sizes.chunk), count)
                ]
                columns = array.at[:, first : first + count]
                copies.append((wanted, pltpu.make_async_copy(columns, place, sems.at[kc, number])))
    return copies


def start_all(copies):
    for wanted, copy in copies:
        copy.start() if wanted is True else pl.when(wanted)(copy.start)


def wait_all(copies):
    for wanted, copy in copies:
        copy.wait() if wanted is True else pl.when(wanted)(copy.wait)


def with_arrays(tiles, arrays):
    arrays = iter(arrays)
    return [
        [[(next(arrays), *piece[1:]) for piece in pieces] for pieces in per_section]
        for per_section in tiles
    ]


def arrays_of(tiles):
    return [piece[0] for per_section in tiles for pieces in per_section for piece in pieces]


def own_panel_kernel(sizes, own, out, held, sem):
    begin = pl.multiple_of(lax.axis_index("sec") * sizes.width, sizes.width)
    copy = pltpu.make_async_copy(own.at[:, pl.ds(begin, sizes.width)], held, sem)
    copy.start()
    copy.wait()
    out[...] = held[...].T


def own_panel(sizes, own):
    return pl.pallas_call(
        functools.partial(own_panel_kernel, sizes),
        out_shape=jax.ShapeDtypeStruct((sizes.width, sizes.rows), jnp.bfloat16),
        in_specs=[HBM],
        out_specs=VMEM,
        scratch_shapes=[
            pltpu.VMEM((sizes.rows, sizes.width), jnp.bfloat16),
            pltpu.SemaphoreType.DMA,
        ],
        compiler_params=PARAMS,
        name="own_panel",
    )(own)


def sent_chunk_kernel(sizes, step, *refs):
    *sent, out, held, sem = refs
    distance = lax.rem(lax.axis_index("sec") - step + sizes.sec, sizes.sec)
    distance = jnp.where(distance == 0, 1, distance)
    copies = [
        (distance == kx, pltpu.make_async_copy(piece, held, sem))
        for kx, piece in enumerate(sent, start=1)
    ]
    start_all(copies)
    wait_all(copies)
    out[...] = held[...].T


def sent_chunk(sizes, step, sent):
    shape = (sizes.rows, sizes.chunk)
    return pl.pallas_call(
        functools.partial(sent_chunk_kernel, sizes, step),
        out_shape=jax.ShapeDtypeStruct(shape[::-1], jnp.bfloat16),
        in_specs=[HBM] * len(sent),
        out_specs=VMEM,
        scratch_shapes=[pltpu.VMEM(shape, jnp.bfloat16), pltpu.SemaphoreType.DMA],
        compiler_params=PARAMS,
        name="sent_chunk",
    )(*sent)


def products_kernel(sizes, step, part, block_rows, state_places, tiles, inverse_tiles, *refs):
    n_blocks, n_states = len(block_rows), len(state_places)
    n_tiles, n_inverse_tiles = len(arrays_of(tiles)), len(arrays_of(inverse_tiles))
    blocks, refs = refs[:n_blocks], refs[n_blocks:]
    states, refs = refs[:n_states], refs[n_states:]
    tiles, refs = with_arrays(tiles, refs[:n_tiles]), refs[n_tiles:]
    inverse_tiles, refs = with_arrays(inverse_tiles, refs[:n_inverse_tiles]), refs[n_inverse_tiles:]
    out, up_first, down_first, *refs = refs
    panel, state, rows, left, block_sems, state_sems, tile_sems = refs
    row_index, sec_index, col_index = (lax.axis_index(a) for a in ("row", "sec", "col"))
    count = sizes.chunk

    first_copies = []
    for number, (kx, kc, offset) in enumerate(state_places):
        first = lax.rem(col_index - kc + sizes.col, sizes.col) * sizes.cols + offset
        if kx is not None:
            first = first + lax.rem(sec_index - kx + sizes.sec, sizes.sec) * sizes.width
        height = states[number].shape[0]
        place = state.at[pl.ds(pl.multiple_of(first, height), height)]
        copy = pltpu.make_async_copy(states[number], place, state_sems.at[number])
        first_copies.append((True, copy))
    for number, (ref, row_of) in enumerate(zip(blocks, block_rows)):
        q, wanted = row_of(row_index, sec_index)
        wanted = wanted & (q >= 0) & (q < sizes.row)
        source = ref if ref.shape[0] == count else ref.at[part * count : (part + 1) * count]
        begin = pl.multiple_of(jnp.clip(q, 0, sizes.row - 1) * sizes.rows, sizes.rows)
        place = panel.at[:, pl.ds(begin, sizes.rows)]
        first_copies.append((wanted, pltpu.make_async_copy(source, place, block_sems.at[number])))
    start_all(first_copies)
    tile_copies = []
    for number, array in enumerate((tiles, inverse_tiles)):
        tile_copies += chosen_copies(sizes, step, array, rows, number * sizes.rows, tile_sems.at[number])
    start_all(tile_copies)

    wait_all(first_copies)
    image = jnp.dot(panel[...], state[...], preferred_element_type=jnp.float32)
    left[:, : sizes.rows] = image.astype(jnp.bfloat16)
    wait_all(tile_copies)
    begin = col_index * sizes.cols + sec_index * sizes.width + part * count
    inverse_panel = rows[sizes.rows :, pl.ds(pl.multiple_of(begin, count), count)]
    left[:, sizes.rows :] = inverse_panel.T
    for d in range(sizes.row):
        place = lax.rem(d - row_index + sizes.row, sizes.row)
        out[place] = jnp.dot(
            left[...],
            rows[:, d * sizes.rows : (d + 1) * sizes.rows],
            preferred_element_type=jnp.float32,
        )
    up_first[...] = out[sizes.row - 1].astype(jnp.bfloat16)
    down_first[...] = out[1].astype(jnp.bfloat16)


def products(sizes, step, part, blocks, states, tiles, inverse_tiles):
    flat = arrays_of(tiles) + arrays_of(inverse_tiles)
    most = max(len(p) for per_section in tiles + inverse_tiles for p in per_section)
    shape = (sizes.row, sizes.chunk, sizes.rows)
    return pl.pallas_call(
        functools.partial(
            products_kernel,
            sizes,
            step,
            part,
            [b[0] for b in blocks],
            [s[0] for s in states],
            with_arrays(tiles, [None] * len(flat)),
            with_arrays(inverse_tiles, [None] * len(flat)),
        ),
        out_shape=[jax.ShapeDtypeStruct(shape, jnp.float32)]
        + [jax.ShapeDtypeStruct(shape[1:], jnp.bfloat16)] * 2,
        in_specs=[HBM] * (len(blocks) + len(states) + len(flat)),
        out_specs=[VMEM] * 3,
        scratch_shapes=[
            pltpu.VMEM((sizes.chunk, sizes.order), jnp.bfloat16),
            pltpu.VMEM((sizes.order, sizes.rows), jnp.bfloat16),
            pltpu.VMEM((2 * sizes.rows, sizes.order), jnp.bfloat16),
            pltpu.VMEM((sizes.chunk, 2 * sizes.rows), jnp.bfloat16),
            pltpu.SemaphoreType.DMA((len(blocks),)),
            pltpu.SemaphoreType.DMA((len(states),)),
            pltpu.SemaphoreType.DMA((2, sizes.col, most)),
        ],
        compiler_params=PARAMS,
        cost_estimate=pl.CostEstimate(
            flops=6 * sizes.rows * sizes.chunk * sizes.order,
            bytes_accessed=6 * sizes.rows * sizes.order + 6 * sizes.chunk * sizes.order,
            transcendentals=0,
        ),
        name="products",
    )(*[b[1] for b in blocks], *[s[1] for s in states], *flat)


def output_kernel(sizes, *refs):
    per_step = sizes.sec * CHUNKS
    out = refs[-1]
    sec_index = lax.axis_index("sec")
    for step in range(sizes.sec):

        @pl.when(sec_index == step)
        def _():
            for kx in range(sizes.sec):
                for k in range(CHUNKS):
                    piece = refs[step * per_step + kx * CHUNKS + k][...]
                    first = lax.rem(sec_index - kx + sizes.sec, sizes.sec) * sizes.width
                    begin = pl.multiple_of(first + k * sizes.chunk, sizes.chunk)
                    out[:, pl.ds(begin, sizes.chunk)] = piece.astype(jnp.float32).T


def output(sizes, pieces):
    return pl.pallas_call(
        functools.partial(output_kernel, sizes),
        out_shape=jax.ShapeDtypeStruct((sizes.rows, sizes.cols), jnp.float32),
        in_specs=[VMEM] * len(pieces),
        out_specs=VMEM,
        compiler_params=PARAMS,
        name="output",
    )(*pieces)


def after(value, *others):
    return lax.optimization_barrier((value, *others))[0]


def always(shift):
    return lambda row, sec: (row + shift, True)


def owning(shift, step, owns):
    return lambda row, sec: (row + shift, (sec == step) == owns)


def further_slots(sizes, up, down, others=()):
    last = sizes.row - 1
    found = []
    for slot in range(1, last):
        if slot == 2:
            up, down = after(up, *others), after(down, *others)
        up = lax.ppermute(up, "row", [(i, i + 1) for i in range(slot, last)])
        down = lax.ppermute(down, "row", [(i, i - 1) for i in range(1, sizes.row - slot)])
        found += [(always(-1 - slot), up), (always(1 + slot), down)]
    return found


def first_slot(sizes, block):
    last = sizes.row - 1
    up = lax.ppermute(block, "row", [(i, i + 1) for i in range(last)])
    down = lax.ppermute(block, "row", [(i, i - 1) for i in range(1, sizes.row)])
    return up, down


def scattered_sum(sizes, partials, gather=None):
    blocks, up_first, down_first = partials
    row_index = lax.axis_index("row")
    last = sizes.row - 1
    up = down = None
    found = []
    for slot in range(last):
        if slot:
            up_block = (blocks[last - slot] + up.astype(jnp.float32)).astype(jnp.bfloat16)
            down_block = (blocks[slot + 1] + down.astype(jnp.float32)).astype(jnp.bfloat16)
        else:
            up_block, down_block = up_first, down_first
        low = slot
        if gather is not None:
            if slot == 0:
                up, down = gather
            if slot < last - 1:
                up_block = jnp.where(row_index <= slot, up_block, up)
                down_block = jnp.where(last - row_index <= slot, down_block, down)
                low = last - 1
        up = lax.ppermute(up_block, "row", [(i, i + 1) for i in range(low + 1)])
        down = lax.ppermute(
            down_block, "row", [(i, i - 1) for i in range(last - low, last + 1)]
        )
        if gather is not None and slot < last - 1:
            found += [(always(-2 - slot), up), (always(2 + slot), down)]
    total = blocks[0] + up.astype(jnp.float32) + down.astype(jnp.float32)
    return total.astype(jnp.bfloat16), found


def local(factors, inverses, sigma_end):
    step_count, rows, cols = factors.shape
    assert step_count == 1
    sizes = Sizes(rows, cols)
    sec_size, col_size, width, chunk_width = sizes.sec, sizes.col, sizes.width, sizes.chunk
    sec_index = lax.axis_index("sec")

    def panel(tile, offset, part=None):
        first = (sec_index + offset) % sec_size * width
        if part is None:
            return lax.dynamic_slice_in_dim(tile, first, width, 1)
        return lax.dynamic_slice_in_dim(tile, first + part * chunk_width, chunk_width, 1)

    factor, inverse = factors[0], inverses[0]

    def over_columns(value):
        return [value] + [exchanged(value, "col", kc) for kc in range(1, col_size)]

    def over_columns(value):
        return [value] + [exchanged(value, "col", kc) for kc in range(1, col_size)]

    def part_of(array, part):
        return array[part * chunk_width : (part + 1) * chunk_width]

    def over_columns(value):
        return [value] + [exchanged(value, "col", kc) for kc in range(1, col_size)]

    def part_of(array, part):
        return array[part * chunk_width : (part + 1) * chunk_width]

    last = sec_size - 1
    is_last = sec_index == last
    sent = [[] for _ in range(sec_size)]
    for part in range(CHUNKS):
        for kx in range(1, sec_size):
            sent[kx].append(exchanged(panel(factor, kx, part), "sec", kx))
    own = own_panel(sizes, factor)
    own_first = first_slot(sizes, own)
    own_factors = [factor] + over_columns(after(factor, *own_first))[1:]
    own_inverses = [inverse] + over_columns(after(inverse, *own_first))[1:]
    states = over_columns(after(sigma_end, own).astype(jnp.bfloat16).T)
    state_pieces = [((None, kc, 0), piece) for kc, piece in enumerate(states)]

    sent = [[after(chunk, *own_first) for chunk in chunks] for chunks in sent]
    other, other_first = [], []
    for part in range(CHUNKS):
        block = sent_chunk(sizes, last, [chunks[part] for chunks in sent[1:]])
        if part:
            block = after(block, *states[1:])
        other.append(block)
        other_first.append(first_slot(sizes, block))
    swapped = [chunk for chunks in sent[1:] for chunk in chunks]
    messages = []
    for kx in range(1, sec_size):
        rest = [panel(factor, kx + j) for j in range(1, sec_size)]
        message = jnp.concatenate([*rest, after(inverse, own)], axis=1)
        messages.append(exchanged(after(message, *swapped), "sec", kx))
    sent_columns = [[over_columns(chunk) for chunk in chunks] for chunks in sent]
    moved = [array for chunks in sent_columns for pieces in chunks for array in pieces[1:]]

    factor_blocks = {}
    for part in range(CHUNKS):
        first = other_first[part]
        up, down = (
            jnp.where(is_last, part_of(mine, part), theirs)
            for mine, theirs in zip(own_first, first)
        )
        factor_blocks[last, part] = [
            (owning(0, last, True), own),
            (owning(-1, last, True), own_first[0]),
            (owning(1, last, True), own_first[1]),
            (owning(0, last, False), other[part]),
            (owning(-1, last, False), first[0]),
            (owning(1, last, False), first[1]),
            *further_slots(
                sizes,
                after(up, *moved),
                after(down, *moved),
                [] if part else [*own_factors[1:], *own_inverses[1:], *other_first[CHUNKS - 1]],
            ),
        ]

    late = [array for part in range(CHUNKS) for _, array in factor_blocks[last, part][-2:]]
    factor_tiles = [[[(tile, (0, cols), None, 0)] for tile in own_factors]]
    inverse_tiles = [[[(tile, (0, cols), None, 0)] for tile in own_inverses]]
    for kx in range(1, sec_size):
        arrived = over_columns(after(messages[kx - 1], *late))
        factor_tiles.append(
            [
                [
                    (sent_columns[kx][part][kc], (0, chunk_width), 0, part * chunk_width)
                    for part in range(CHUNKS)
                ]
                + [
                    (arrived[kc], ((j - 1) * width, width), j, 0)
                    for j in range(1, sec_size)
                ]
                for kc in range(col_size)
            ]
        )
        inverse_tiles.append([[(tile, (last * width, cols), None, 0)] for tile in arrived])

    results = {}
    for step in reversed(range(sec_size)):
        next_pieces = []
        for part in range(CHUNKS):
            if step == last and sec_size == 2:
                ahead = tuple(
                    jnp.where(is_last, theirs, part_of(mine, part))
                    for mine, theirs in zip(own_first, other_first[part])
                )
                started = [
                    (owning(0, last, True), other[part]),
                    (owning(-1, last, True), other_first[part][0]),
                    (owning(1, last, True), other_first[part][1]),
                    (owning(0, last, False), own),
                    (owning(-1, last, False), own_first[0]),
                    (owning(1, last, False), own_first[1]),
                ]
            elif step:
                earlier = [array for _, array in factor_blocks[step, part][-2:]]
                mine = sent_chunk(sizes, step - 1, [chunks[part] for chunks in sent[1:]])
                block = after(jnp.where(sec_index == step - 1, part_of(own, part), mine), *earlier)
                ahead = first_slot(sizes, block)
                started = [(always(0), block), (always(-1), ahead[0]), (always(1), ahead[1])]
            partials = products(
                sizes, step, part, factor_blocks[step, part], state_pieces, factor_tiles, inverse_tiles
            )
            if step:
                total, found = scattered_sum(sizes, partials, ahead)
                factor_blocks[step - 1, part] = started + found
            else:
                total, _ = scattered_sum(sizes, partials)
            for kx in range(sec_size):
                piece = exchanged(total, "sec", kx) if kx else total
                results[step, kx, part] = piece
                if step:
                    for kc, moved in enumerate(over_columns(piece)):
                        next_pieces.append(((kx, kc, part * chunk_width), moved))
        state_pieces = next_pieces

    return output(
        sizes,
        [
            results[step, kx, part]
            for step in range(sec_size)
            for kx in range(sec_size)
            for part in range(CHUNKS)
        ],
    )[None]


def solution(mesh):
    in_specs = (
        P(("groups", "sec"), "row", "col"),
        P(("groups", "sec"), "row", "col"),
        P(("groups", "row"), "col"),
    )
    out_specs = P(("groups", "sec"), "row", "col")
    return jax.shard_map(local, mesh=mesh, in_specs=in_specs, out_specs=out_specs, check_vma=False)
```

```python
import functools

import jax
import jax.numpy as jnp
from jax import lax
from jax.experimental import pallas as pl
from jax.experimental.pallas import tpu as pltpu
from jax.sharding import PartitionSpec as P

CHUNKS = 2
ANY = pl.BlockSpec(memory_space=pl.ANY)
VMEM = pl.BlockSpec(memory_space=pltpu.VMEM)
PARAMS = pltpu.CompilerParams(vmem_limit_bytes=12 * 1024 * 1024)


def exchanged(value, axis, steps):
    count = lax.axis_size(axis)
    return lax.ppermute(value, axis, [(i, (i + steps) % count) for i in range(count)])


class Sizes:
    def __init__(self, rows, cols):
        self.row = lax.axis_size("row")
        self.sec = lax.axis_size("sec")
        self.col = lax.axis_size("col")
        self.rows = rows
        self.cols = cols
        self.order = cols * self.col
        self.width = cols // self.sec
        self.chunk = self.width // CHUNKS
        self.per_tile = self.row // self.col


def chosen_copies(sizes, step, tiles, target, top, sems):
    sec_index, col_index = lax.axis_index("sec"), lax.axis_index("col")
    copies = []
    for kc in range(sizes.col):
        begin = lax.rem(col_index - kc + sizes.col, sizes.col) * sizes.cols
        place = target.at[top : top + sizes.rows, pl.ds(pl.multiple_of(begin, sizes.cols), sizes.cols)]
        for kx in range(sizes.sec):
            copy = pltpu.make_async_copy(tiles[kx][kc], place, sems.at[kc])
            wanted = lax.rem(sec_index - kx + sizes.sec, sizes.sec) == step
            copies.append((wanted, copy))
    return copies


def start_all(copies):
    for wanted, copy in copies:
        copy.start() if wanted is True else pl.when(wanted)(copy.start)


def wait_all(copies):
    for wanted, copy in copies:
        copy.wait() if wanted is True else pl.when(wanted)(copy.wait)


def nested(refs, sizes):
    return [refs[kx * sizes.col : (kx + 1) * sizes.col] for kx in range(sizes.sec)]


def panel_kernel(sizes, step, offset, own, *refs):
    *sent, out, held, sem = refs
    sec_index = lax.axis_index("sec")
    count = out.shape[0]
    begin = pl.multiple_of(sec_index * sizes.width + offset, sizes.chunk)
    copies = [(sec_index == step, pltpu.make_async_copy(own.at[:, pl.ds(begin, count)], held, sem))]
    per_section = len(sent) // (sizes.sec - 1)
    for kx in range(1, sizes.sec):
        wanted = lax.rem(sec_index - kx + sizes.sec, sizes.sec) == step
        pieces = sent[(kx - 1) * per_section : kx * per_section]
        height = count // per_section
        for k, piece in enumerate(pieces):
            target = held.at[:, k * height : (k + 1) * height]
            copies.append((wanted, pltpu.make_async_copy(piece, target, sem)))
    start_all(copies)
    wait_all(copies)
    out[...] = held[...].T


def transposed_panel(sizes, step, own, sent, part=None):
    count = sizes.width if part is None else sizes.chunk
    offset = 0 if part is None else part * sizes.chunk
    flat = [piece for pieces in sent for piece in pieces]
    return pl.pallas_call(
        functools.partial(panel_kernel, sizes, step, offset),
        out_shape=jax.ShapeDtypeStruct((count, sizes.rows), jnp.bfloat16),
        in_specs=[ANY] + [VMEM] * len(flat),
        out_specs=VMEM,
        scratch_shapes=[
            pltpu.VMEM((sizes.rows, count), jnp.bfloat16),
            pltpu.SemaphoreType.DMA,
        ],
        compiler_params=PARAMS,
        name="panel",
    )(own, *flat)


def products_kernel(sizes, step, part, block_rows, state_places, *refs):
    n_blocks, n_states, n_tiles = len(block_rows), len(state_places), sizes.sec * sizes.col
    blocks, refs = refs[:n_blocks], refs[n_blocks:]
    states, refs = refs[:n_states], refs[n_states:]
    tiles, refs = nested(refs[:n_tiles], sizes), refs[n_tiles:]
    inverse_tiles, refs = nested(refs[:n_tiles], sizes), refs[n_tiles:]
    out, up_first, down_first, *refs = refs
    panel, state, rows, left, block_sems, state_sems, tile_sems = refs
    row_index, sec_index, col_index = (lax.axis_index(a) for a in ("row", "sec", "col"))
    count = sizes.chunk

    first_copies = []
    for number, (kx, kc, offset) in enumerate(state_places):
        first = lax.rem(col_index - kc + sizes.col, sizes.col) * sizes.cols + offset
        if kx is not None:
            first = first + lax.rem(sec_index - kx + sizes.sec, sizes.sec) * sizes.width
        height = states[number].shape[0]
        place = state.at[pl.ds(pl.multiple_of(first, height), height)]
        copy = pltpu.make_async_copy(states[number], place, state_sems.at[number])
        first_copies.append((True, copy))
    for number, (ref, row_of) in enumerate(zip(blocks, block_rows)):
        q, low, high = row_of(row_index)
        wanted = (q >= low) & (q <= high)
        source = ref if ref.shape[0] == count else ref.at[part * count : (part + 1) * count]
        begin = pl.multiple_of(jnp.clip(q, 0, sizes.row - 1) * sizes.rows, sizes.rows)
        place = panel.at[:, pl.ds(begin, sizes.rows)]
        first_copies.append((wanted, pltpu.make_async_copy(source, place, block_sems.at[number])))
    start_all(first_copies)
    tile_copies = []
    for number, array in enumerate((tiles, inverse_tiles)):
        tile_copies += chosen_copies(sizes, step, array, rows, number * sizes.rows, tile_sems.at[number])
    start_all(tile_copies)

    wait_all(first_copies)
    image = jnp.dot(panel[...], state[...], preferred_element_type=jnp.float32)
    left[:, : sizes.rows] = image.astype(jnp.bfloat16)
    wait_all(tile_copies)
    begin = col_index * sizes.cols + sec_index * sizes.width + part * count
    inverse_panel = rows[sizes.rows :, pl.ds(pl.multiple_of(begin, count), count)]
    left[:, sizes.rows :] = inverse_panel.T
    for d in range(sizes.row):
        place = lax.rem(d - row_index + sizes.row, sizes.row)
        out[place] = jnp.dot(
            left[...],
            rows[:, d * sizes.rows : (d + 1) * sizes.rows],
            preferred_element_type=jnp.float32,
        )
    up_first[...] = out[sizes.row - 1].astype(jnp.bfloat16)
    down_first[...] = out[1].astype(jnp.bfloat16)


def products(sizes, step, part, blocks, states, tiles, inverse_tiles):
    flat = [tile for per_section in tiles + inverse_tiles for tile in per_section]
    shape = (sizes.row, sizes.chunk, sizes.rows)
    return pl.pallas_call(
        functools.partial(
            products_kernel, sizes, step, part, [b[0] for b in blocks], [s[0] for s in states]
        ),
        out_shape=[jax.ShapeDtypeStruct(shape, jnp.float32)]
        + [jax.ShapeDtypeStruct(shape[1:], jnp.bfloat16)] * 2,
        in_specs=[VMEM] * len(blocks) + [ANY] * (len(states) + len(flat)),
        out_specs=[VMEM] * 3,
        scratch_shapes=[
            pltpu.VMEM((sizes.chunk, sizes.order), jnp.bfloat16),
            pltpu.VMEM((sizes.order, sizes.rows), jnp.bfloat16),
            pltpu.VMEM((2 * sizes.rows, sizes.order), jnp.bfloat16),
            pltpu.VMEM((sizes.chunk, 2 * sizes.rows), jnp.bfloat16),
            pltpu.SemaphoreType.DMA((len(blocks),)),
            pltpu.SemaphoreType.DMA((len(states),)),
            pltpu.SemaphoreType.DMA((2, sizes.col)),
        ],
        compiler_params=PARAMS,
        cost_estimate=pl.CostEstimate(
            flops=6 * sizes.rows * sizes.chunk * sizes.order,
            bytes_accessed=6 * sizes.rows * sizes.order + 6 * sizes.chunk * sizes.order,
            transcendentals=0,
        ),
        name="products",
    )(*[b[1] for b in blocks], *[s[1] for s in states], *flat)


def output_kernel(sizes, *refs):
    per_step = sizes.sec * CHUNKS
    out = refs[-1]
    sec_index = lax.axis_index("sec")
    for step in range(sizes.sec):

        @pl.when(sec_index == step)
        def _():
            for kx in range(sizes.sec):
                for k in range(CHUNKS):
                    piece = refs[step * per_step + kx * CHUNKS + k][...]
                    first = lax.rem(sec_index - kx + sizes.sec, sizes.sec) * sizes.width
                    begin = pl.multiple_of(first + k * sizes.chunk, sizes.chunk)
                    out[:, pl.ds(begin, sizes.chunk)] = piece.astype(jnp.float32).T


def output(sizes, pieces):
    return pl.pallas_call(
        functools.partial(output_kernel, sizes),
        out_shape=jax.ShapeDtypeStruct((sizes.rows, sizes.cols), jnp.float32),
        in_specs=[VMEM] * len(pieces),
        out_specs=VMEM,
        compiler_params=PARAMS,
        name="output",
    )(*pieces)


def after(value, *others):
    return lax.optimization_barrier((value, *others))[0]


def neighbours_gathered(sizes, block):
    last = sizes.row - 1
    up = down = block
    found = [(lambda row: (row, 0, last), block)]
    for slot in range(last):
        up = lax.ppermute(up, "row", [(i, i + 1) for i in range(slot, last)])
        down = lax.ppermute(down, "row", [(i, i - 1) for i in range(1, sizes.row - slot)])
        found.append((lambda row, slot=slot: (row - 1 - slot, 0, last), up))
        found.append((lambda row, slot=slot: (row + 1 + slot, 0, last), down))
    return found


def first_slot(sizes, block):
    last = sizes.row - 1
    up = lax.ppermute(block, "row", [(i, i + 1) for i in range(last)])
    down = lax.ppermute(block, "row", [(i, i - 1) for i in range(1, sizes.row)])
    return up, down


def scattered_sum(sizes, partials, gather=None):
    blocks, up_first, down_first = partials
    row_index = lax.axis_index("row")
    last = sizes.row - 1
    up = down = None
    found = []
    for slot in range(last):
        if slot:
            up_block = (blocks[last - slot] + up.astype(jnp.float32)).astype(jnp.bfloat16)
            down_block = (blocks[slot + 1] + down.astype(jnp.float32)).astype(jnp.bfloat16)
        else:
            up_block, down_block = up_first, down_first
        low = slot
        if gather is not None:
            if slot == 0:
                up, down = gather
            if slot < last - 1:
                up_block = jnp.where(row_index <= slot, up_block, up)
                down_block = jnp.where(last - row_index <= slot, down_block, down)
                low = last - 1
        up = lax.ppermute(up_block, "row", [(i, i + 1) for i in range(low + 1)])
        down = lax.ppermute(
            down_block, "row", [(i, i - 1) for i in range(last - low, last + 1)]
        )
        if gather is not None and slot < last - 1:
            found.append((lambda row, slot=slot: (row - 2 - slot, 0, last), up))
            found.append((lambda row, slot=slot: (row + 2 + slot, 0, last), down))
    total = blocks[0] + up.astype(jnp.float32) + down.astype(jnp.float32)
    return total.astype(jnp.bfloat16), found


def local(factors, inverses, sigma_end):
    step_count, rows, cols = factors.shape
    assert step_count == 1
    sizes = Sizes(rows, cols)
    sec_size, col_size, width, chunk = sizes.sec, sizes.col, sizes.width, sizes.chunk
    sec_index = lax.axis_index("sec")

    def panel(tile, offset, part=None):
        first = (sec_index + offset) % sec_size * width
        if part is None:
            return lax.dynamic_slice_in_dim(tile, first, width, 1)
        return lax.dynamic_slice_in_dim(tile, first + part * chunk, chunk, 1)

    factor, inverse = factors[0], inverses[0]

    arrived_chunks = [None]
    for kx in range(1, sec_size):
        arrived_chunks.append(
            [exchanged(panel(factor, kx, part), "sec", kx) for part in range(CHUNKS)]
        )

    factor_blocks = {}
    last = sec_size - 1
    for part in range(CHUNKS):
        sent = [[chunks[part]] for chunks in arrived_chunks[1:]]
        block = transposed_panel(sizes, last, factor, sent, part)
        factor_blocks[last, part] = neighbours_gathered(sizes, block)
    swapped = [chunk for chunks in arrived_chunks[1:] for chunk in chunks]

    def tiles_over_sections(tile, first_chunks):
        found = [tile]
        for kx in range(1, sec_size):
            whole = jnp.zeros_like(tile)
            for j in range(sec_size):
                if j == 0 and first_chunks is not None:
                    piece = jnp.concatenate(first_chunks[kx], axis=1)
                else:
                    piece = exchanged(after(panel(tile, kx + j), *swapped), "sec", kx)
                first = (sec_index + j) % sec_size * width
                whole = lax.dynamic_update_slice_in_dim(whole, piece, first, 1)
            found.append(whole)
        return found

    def over_columns(value):
        return [value] + [exchanged(value, "col", kc) for kc in range(1, col_size)]

    state_pieces = [
        ((None, kc, 0), piece)
        for kc, piece in enumerate(over_columns(sigma_end.astype(jnp.bfloat16).T))
    ]
    factor_tiles = [over_columns(tile) for tile in tiles_over_sections(factor, arrived_chunks)]
    inverse_tiles = [
        over_columns(tile)
        for tile in [inverse]
        + [exchanged(after(inverse, *swapped), "sec", kx) for kx in range(1, sec_size)]
    ]

    results = {}
    for step in reversed(range(sec_size)):
        trailing = []
        if step:
            earlier = [array for k in range(CHUNKS) for _, array in factor_blocks[step, k][-2:]]
            for part in range(CHUNKS):
                sent = [[chunks[part]] for chunks in arrived_chunks[1:]]
                block = after(transposed_panel(sizes, step - 1, factor, sent, part), *earlier)
                trailing.append((block, first_slot(sizes, block)))
        next_pieces = []
        for part in range(CHUNKS):
            partials = products(
                sizes, step, part, factor_blocks[step, part], state_pieces, factor_tiles, inverse_tiles
            )
            if step:
                block, (up, down) = trailing[part]
                total, found = scattered_sum(sizes, partials, (up, down))
                edge = sizes.row - 1
                factor_blocks[step - 1, part] = [
                    (lambda row: (row, 0, edge), block),
                    (lambda row: (row - 1, 0, edge), up),
                    (lambda row: (row + 1, 0, edge), down),
                    *found,
                ]
            else:
                total, _ = scattered_sum(sizes, partials)
            for kx in range(sec_size):
                piece = exchanged(total, "sec", kx) if kx else total
                results[step, kx, part] = piece
                if step:
                    for kc, moved in enumerate(over_columns(piece)):
                        next_pieces.append(((kx, kc, part * chunk), moved))
        state_pieces = next_pieces

    return output(
        sizes,
        [
            results[step, kx, part]
            for step in range(sec_size)
            for kx in range(sec_size)
            for part in range(CHUNKS)
        ],
    )[None]


def solution(mesh):
    in_specs = (
        P(("groups", "sec"), "row", "col"),
        P(("groups", "sec"), "row", "col"),
        P(("groups", "row"), "col"),
    )
    out_specs = P(("groups", "sec"), "row", "col")
    return jax.shard_map(local, mesh=mesh, in_specs=in_specs, out_specs=out_specs, check_vma=False)
```

```python
import functools

import jax
import jax.numpy as jnp
from jax import lax
from jax.experimental import pallas as pl
from jax.experimental.pallas import tpu as pltpu
from jax.sharding import PartitionSpec as P

CHUNKS = 2
ANY = pl.BlockSpec(memory_space=pl.ANY)
VMEM = pl.BlockSpec(memory_space=pltpu.VMEM)
PARAMS = pltpu.CompilerParams(vmem_limit_bytes=12 * 1024 * 1024)


def exchanged(value, axis, steps):
    count = lax.axis_size(axis)
    return lax.ppermute(value, axis, [(i, (i + steps) % count) for i in range(count)])


class Sizes:
    def __init__(self, rows, cols):
        self.row = lax.axis_size("row")
        self.sec = lax.axis_size("sec")
        self.col = lax.axis_size("col")
        self.rows = rows
        self.cols = cols
        self.order = cols * self.col
        self.width = cols // self.sec
        self.chunk = self.width // CHUNKS
        self.per_tile = self.row // self.col


def chosen_copies(sizes, step, tiles, target, top, sems):
    sec_index, col_index = lax.axis_index("sec"), lax.axis_index("col")
    copies = []
    for kc in range(sizes.col):
        begin = lax.rem(col_index - kc + sizes.col, sizes.col) * sizes.cols
        place = target.at[top : top + sizes.rows, pl.ds(pl.multiple_of(begin, sizes.cols), sizes.cols)]
        for kx in range(sizes.sec):
            copy = pltpu.make_async_copy(tiles[kx][kc], place, sems.at[kc])
            wanted = lax.rem(sec_index - kx + sizes.sec, sizes.sec) == step
            copies.append((wanted, copy))
    return copies


def start_all(copies):
    for wanted, copy in copies:
        copy.start() if wanted is True else pl.when(wanted)(copy.start)


def wait_all(copies):
    for wanted, copy in copies:
        copy.wait() if wanted is True else pl.when(wanted)(copy.wait)


def nested(refs, sizes):
    return [refs[kx * sizes.col : (kx + 1) * sizes.col] for kx in range(sizes.sec)]


def panel_kernel(sizes, step, offset, own, *refs):
    *sent, out, held, sem = refs
    sec_index = lax.axis_index("sec")
    count = out.shape[0]
    begin = pl.multiple_of(sec_index * sizes.width + offset, sizes.chunk)
    copies = [(sec_index == step, pltpu.make_async_copy(own.at[:, pl.ds(begin, count)], held, sem))]
    per_section = len(sent) // (sizes.sec - 1)
    for kx in range(1, sizes.sec):
        wanted = lax.rem(sec_index - kx + sizes.sec, sizes.sec) == step
        pieces = sent[(kx - 1) * per_section : kx * per_section]
        height = count // per_section
        for k, piece in enumerate(pieces):
            target = held.at[:, k * height : (k + 1) * height]
            copies.append((wanted, pltpu.make_async_copy(piece, target, sem)))
    start_all(copies)
    wait_all(copies)
    out[...] = held[...].T


def transposed_panel(sizes, step, own, sent, part=None):
    count = sizes.width if part is None else sizes.chunk
    offset = 0 if part is None else part * sizes.chunk
    flat = [piece for pieces in sent for piece in pieces]
    return pl.pallas_call(
        functools.partial(panel_kernel, sizes, step, offset),
        out_shape=jax.ShapeDtypeStruct((count, sizes.rows), jnp.bfloat16),
        in_specs=[ANY] + [VMEM] * len(flat),
        out_specs=VMEM,
        scratch_shapes=[
            pltpu.VMEM((sizes.rows, count), jnp.bfloat16),
            pltpu.SemaphoreType.DMA,
        ],
        compiler_params=PARAMS,
        name="panel",
    )(own, *flat)


def products_kernel(sizes, step, part, block_rows, state_places, *refs):
    n_blocks, n_states, n_tiles = len(block_rows), len(state_places), sizes.sec * sizes.col
    blocks, refs = refs[:n_blocks], refs[n_blocks:]
    states, refs = refs[:n_states], refs[n_states:]
    tiles, refs = nested(refs[:n_tiles], sizes), refs[n_tiles:]
    inverse_tiles, refs = nested(refs[:n_tiles], sizes), refs[n_tiles:]
    out, up_first, down_first, *refs = refs
    panel, state, rows, left, block_sems, state_sems, tile_sems = refs
    row_index, sec_index, col_index = (lax.axis_index(a) for a in ("row", "sec", "col"))
    count = sizes.chunk

    first_copies = []
    for number, (kx, kc, offset) in enumerate(state_places):
        first = lax.rem(col_index - kc + sizes.col, sizes.col) * sizes.cols + offset
        if kx is not None:
            first = first + lax.rem(sec_index - kx + sizes.sec, sizes.sec) * sizes.width
        height = states[number].shape[0]
        place = state.at[pl.ds(pl.multiple_of(first, height), height)]
        copy = pltpu.make_async_copy(states[number], place, state_sems.at[number])
        first_copies.append((True, copy))
    for number, (ref, row_of) in enumerate(zip(blocks, block_rows)):
        q, low, high = row_of(row_index)
        wanted = (q >= low) & (q <= high)
        source = ref if ref.shape[0] == count else ref.at[part * count : (part + 1) * count]
        begin = pl.multiple_of(jnp.clip(q, 0, sizes.row - 1) * sizes.rows, sizes.rows)
        place = panel.at[:, pl.ds(begin, sizes.rows)]
        first_copies.append((wanted, pltpu.make_async_copy(source, place, block_sems.at[number])))
    start_all(first_copies)
    tile_copies = []
    for number, array in enumerate((tiles, inverse_tiles)):
        tile_copies += chosen_copies(sizes, step, array, rows, number * sizes.rows, tile_sems.at[number])
    start_all(tile_copies)

    wait_all(first_copies)
    image = jnp.dot(panel[...], state[...], preferred_element_type=jnp.float32)
    left[:, : sizes.rows] = image.astype(jnp.bfloat16)
    wait_all(tile_copies)
    begin = col_index * sizes.cols + sec_index * sizes.width + part * count
    inverse_panel = rows[sizes.rows :, pl.ds(pl.multiple_of(begin, count), count)]
    left[:, sizes.rows :] = inverse_panel.T
    for d in range(sizes.row):
        place = lax.rem(d - row_index + sizes.row, sizes.row)
        out[place] = jnp.dot(
            left[...],
            rows[:, d * sizes.rows : (d + 1) * sizes.rows],
            preferred_element_type=jnp.float32,
        )
    up_first[...] = out[sizes.row - 1].astype(jnp.bfloat16)
    down_first[...] = out[1].astype(jnp.bfloat16)


def products(sizes, step, part, blocks, states, tiles, inverse_tiles):
    flat = [tile for per_section in tiles + inverse_tiles for tile in per_section]
    shape = (sizes.row, sizes.chunk, sizes.rows)
    return pl.pallas_call(
        functools.partial(
            products_kernel, sizes, step, part, [b[0] for b in blocks], [s[0] for s in states]
        ),
        out_shape=[jax.ShapeDtypeStruct(shape, jnp.float32)]
        + [jax.ShapeDtypeStruct(shape[1:], jnp.bfloat16)] * 2,
        in_specs=[VMEM] * len(blocks) + [ANY] * (len(states) + len(flat)),
        out_specs=[VMEM] * 3,
        scratch_shapes=[
            pltpu.VMEM((sizes.chunk, sizes.order), jnp.bfloat16),
            pltpu.VMEM((sizes.order, sizes.rows), jnp.bfloat16),
            pltpu.VMEM((2 * sizes.rows, sizes.order), jnp.bfloat16),
            pltpu.VMEM((sizes.chunk, 2 * sizes.rows), jnp.bfloat16),
            pltpu.SemaphoreType.DMA((len(blocks),)),
            pltpu.SemaphoreType.DMA((len(states),)),
            pltpu.SemaphoreType.DMA((2, sizes.col)),
        ],
        compiler_params=PARAMS,
        cost_estimate=pl.CostEstimate(
            flops=6 * sizes.rows * sizes.chunk * sizes.order,
            bytes_accessed=6 * sizes.rows * sizes.order + 6 * sizes.chunk * sizes.order,
            transcendentals=0,
        ),
        name="products",
    )(*[b[1] for b in blocks], *[s[1] for s in states], *flat)


def output_kernel(sizes, *refs):
    per_step = sizes.sec * CHUNKS
    out = refs[-1]
    sec_index = lax.axis_index("sec")
    for step in range(sizes.sec):

        @pl.when(sec_index == step)
        def _():
            for kx in range(sizes.sec):
                for k in range(CHUNKS):
                    piece = refs[step * per_step + kx * CHUNKS + k][...]
                    first = lax.rem(sec_index - kx + sizes.sec, sizes.sec) * sizes.width
                    begin = pl.multiple_of(first + k * sizes.chunk, sizes.chunk)
                    out[:, pl.ds(begin, sizes.chunk)] = piece.astype(jnp.float32).T


def output(sizes, pieces):
    return pl.pallas_call(
        functools.partial(output_kernel, sizes),
        out_shape=jax.ShapeDtypeStruct((sizes.rows, sizes.cols), jnp.float32),
        in_specs=[VMEM] * len(pieces),
        out_specs=VMEM,
        compiler_params=PARAMS,
        name="output",
    )(*pieces)


def after(value, *others):
    return lax.optimization_barrier((value, *others))[0]


def neighbours_gathered(sizes, block):
    last = sizes.row - 1
    up = down = block
    found = [(lambda row: (row, 0, last), block)]
    for slot in range(last):
        up = lax.ppermute(up, "row", [(i, i + 1) for i in range(slot, last)])
        down = lax.ppermute(down, "row", [(i, i - 1) for i in range(1, sizes.row - slot)])
        found.append((lambda row, slot=slot: (row - 1 - slot, 0, last), up))
        found.append((lambda row, slot=slot: (row + 1 + slot, 0, last), down))
    return found


def first_slot(sizes, block):
    last = sizes.row - 1
    up = lax.ppermute(block, "row", [(i, i + 1) for i in range(last)])
    down = lax.ppermute(block, "row", [(i, i - 1) for i in range(1, sizes.row)])
    return up, down


def scattered_sum(sizes, partials, gather=None):
    blocks, up_first, down_first = partials
    row_index = lax.axis_index("row")
    last = sizes.row - 1
    up = down = None
    found = []
    for slot in range(last):
        if slot:
            up_block = (blocks[last - slot] + up.astype(jnp.float32)).astype(jnp.bfloat16)
            down_block = (blocks[slot + 1] + down.astype(jnp.float32)).astype(jnp.bfloat16)
        else:
            up_block, down_block = up_first, down_first
        low = slot
        if gather is not None:
            if slot == 0:
                up, down = gather
            if slot < last - 1:
                up_block = jnp.where(row_index <= slot, up_block, up)
                down_block = jnp.where(last - row_index <= slot, down_block, down)
                low = last - 1
        up = lax.ppermute(up_block, "row", [(i, i + 1) for i in range(low + 1)])
        down = lax.ppermute(
            down_block, "row", [(i, i - 1) for i in range(last - low, last + 1)]
        )
        if gather is not None and slot < last - 1:
            found.append((lambda row, slot=slot: (row - 2 - slot, 0, last), up))
            found.append((lambda row, slot=slot: (row + 2 + slot, 0, last), down))
    total = blocks[0] + up.astype(jnp.float32) + down.astype(jnp.float32)
    return total.astype(jnp.bfloat16), found


def local(factors, inverses, sigma_end):
    step_count, rows, cols = factors.shape
    assert step_count == 1
    sizes = Sizes(rows, cols)
    sec_size, col_size, width, chunk = sizes.sec, sizes.col, sizes.width, sizes.chunk
    sec_index = lax.axis_index("sec")

    def panel(tile, offset, part=None):
        first = (sec_index + offset) % sec_size * width
        if part is None:
            return lax.dynamic_slice_in_dim(tile, first, width, 1)
        return lax.dynamic_slice_in_dim(tile, first + part * chunk, chunk, 1)

    factor, inverse = factors[0], inverses[0]

    arrived_chunks = [None]
    for kx in range(1, sec_size):
        arrived_chunks.append(
            [exchanged(panel(factor, kx, part), "sec", kx) for part in range(CHUNKS)]
        )

    factor_blocks = {}
    last = sec_size - 1
    for part in range(CHUNKS):
        sent = [[chunks[part]] for chunks in arrived_chunks[1:]]
        block = transposed_panel(sizes, last, factor, sent, part)
        factor_blocks[last, part] = neighbours_gathered(sizes, block)
    swapped = [chunk for chunks in arrived_chunks[1:] for chunk in chunks]

    def tiles_over_sections(tile, first_chunks):
        found = [tile]
        for kx in range(1, sec_size):
            whole = jnp.zeros_like(tile)
            for j in range(sec_size):
                if j == 0 and first_chunks is not None:
                    piece = jnp.concatenate(first_chunks[kx], axis=1)
                else:
                    piece = exchanged(after(panel(tile, kx + j), *swapped), "sec", kx)
                first = (sec_index + j) % sec_size * width
                whole = lax.dynamic_update_slice_in_dim(whole, piece, first, 1)
            found.append(whole)
        return found

    def over_columns(value):
        return [value] + [exchanged(value, "col", kc) for kc in range(1, col_size)]

    state_pieces = [
        ((None, kc, 0), piece)
        for kc, piece in enumerate(over_columns(sigma_end.astype(jnp.bfloat16).T))
    ]
    factor_tiles = [over_columns(tile) for tile in tiles_over_sections(factor, arrived_chunks)]
    inverse_tiles = [
        over_columns(tile)
        for tile in [inverse]
        + [exchanged(after(inverse, *swapped), "sec", kx) for kx in range(1, sec_size)]
    ]

    results = {}
    for step in reversed(range(sec_size)):
        next_pieces = []
        for part in range(CHUNKS):
            if step:
                earlier = [array for k in range(CHUNKS) for _, array in factor_blocks[step, k][-2:]]
                if part:
                    earlier += partials[1:]
                sent = [[chunks[part]] for chunks in arrived_chunks[1:]]
                block = after(transposed_panel(sizes, step - 1, factor, sent, part), *earlier)
                up, down = first_slot(sizes, block)
            partials = products(
                sizes, step, part, factor_blocks[step, part], state_pieces, factor_tiles, inverse_tiles
            )
            if step:
                total, found = scattered_sum(sizes, partials, (up, down))
                edge = sizes.row - 1
                factor_blocks[step - 1, part] = [
                    (lambda row: (row, 0, edge), block),
                    (lambda row: (row - 1, 0, edge), up),
                    (lambda row: (row + 1, 0, edge), down),
                    *found,
                ]
            else:
                total, _ = scattered_sum(sizes, partials)
            for kx in range(sec_size):
                piece = exchanged(total, "sec", kx) if kx else total
                results[step, kx, part] = piece
                if step:
                    for kc, moved in enumerate(over_columns(piece)):
                        next_pieces.append(((kx, kc, part * chunk), moved))
        state_pieces = next_pieces

    return output(
        sizes,
        [
            results[step, kx, part]
            for step in range(sec_size)
            for kx in range(sec_size)
            for part in range(CHUNKS)
        ],
    )[None]


def solution(mesh):
    in_specs = (
        P(("groups", "sec"), "row", "col"),
        P(("groups", "sec"), "row", "col"),
        P(("groups", "row"), "col"),
    )
    out_specs = P(("groups", "sec"), "row", "col")
    return jax.shard_map(local, mesh=mesh, in_specs=in_specs, out_specs=out_specs, check_vma=False)
```

```python
import functools

import jax
import jax.numpy as jnp
from jax import lax
from jax.experimental import pallas as pl
from jax.experimental.pallas import tpu as pltpu
from jax.sharding import PartitionSpec as P

CHUNKS = 2
ANY = pl.BlockSpec(memory_space=pl.ANY)
VMEM = pl.BlockSpec(memory_space=pltpu.VMEM)
PARAMS = pltpu.CompilerParams(vmem_limit_bytes=12 * 1024 * 1024)


def exchanged(value, axis, steps):
    count = lax.axis_size(axis)
    return lax.ppermute(value, axis, [(i, (i + steps) % count) for i in range(count)])


class Sizes:
    def __init__(self, rows, cols):
        self.row = lax.axis_size("row")
        self.sec = lax.axis_size("sec")
        self.col = lax.axis_size("col")
        self.rows = rows
        self.cols = cols
        self.order = cols * self.col
        self.width = cols // self.sec
        self.chunk = self.width // CHUNKS
        self.per_tile = self.row // self.col


def chosen_copies(sizes, step, tiles, target, top, sems):
    sec_index, col_index = lax.axis_index("sec"), lax.axis_index("col")
    copies = []
    for kc in range(sizes.col):
        begin = lax.rem(col_index - kc + sizes.col, sizes.col) * sizes.cols
        place = target.at[top : top + sizes.rows, pl.ds(pl.multiple_of(begin, sizes.cols), sizes.cols)]
        for kx in range(sizes.sec):
            copy = pltpu.make_async_copy(tiles[kx][kc], place, sems.at[kc])
            wanted = lax.rem(sec_index - kx + sizes.sec, sizes.sec) == step
            copies.append((wanted, copy))
    return copies


def start_all(copies):
    for wanted, copy in copies:
        copy.start() if wanted is True else pl.when(wanted)(copy.start)


def wait_all(copies):
    for wanted, copy in copies:
        copy.wait() if wanted is True else pl.when(wanted)(copy.wait)


def nested(refs, sizes):
    return [refs[kx * sizes.col : (kx + 1) * sizes.col] for kx in range(sizes.sec)]


def panel_kernel(sizes, step, offset, own, *refs):
    *sent, out, held, sem = refs
    sec_index = lax.axis_index("sec")
    count = out.shape[0]
    begin = pl.multiple_of(sec_index * sizes.width + offset, sizes.chunk)
    copies = [(sec_index == step, pltpu.make_async_copy(own.at[:, pl.ds(begin, count)], held, sem))]
    per_section = len(sent) // (sizes.sec - 1)
    for kx in range(1, sizes.sec):
        wanted = lax.rem(sec_index - kx + sizes.sec, sizes.sec) == step
        pieces = sent[(kx - 1) * per_section : kx * per_section]
        height = count // per_section
        for k, piece in enumerate(pieces):
            target = held.at[:, k * height : (k + 1) * height]
            copies.append((wanted, pltpu.make_async_copy(piece, target, sem)))
    start_all(copies)
    wait_all(copies)
    out[...] = held[...].T


def transposed_panel(sizes, step, own, sent, part=None):
    count = sizes.width if part is None else sizes.chunk
    offset = 0 if part is None else part * sizes.chunk
    flat = [piece for pieces in sent for piece in pieces]
    return pl.pallas_call(
        functools.partial(panel_kernel, sizes, step, offset),
        out_shape=jax.ShapeDtypeStruct((count, sizes.rows), jnp.bfloat16),
        in_specs=[ANY] + [VMEM] * len(flat),
        out_specs=VMEM,
        scratch_shapes=[
            pltpu.VMEM((sizes.rows, count), jnp.bfloat16),
            pltpu.SemaphoreType.DMA,
        ],
        compiler_params=PARAMS,
        name="panel",
    )(own, *flat)


def products_kernel(sizes, step, part, block_rows, state_places, *refs):
    n_blocks, n_states, n_tiles = len(block_rows), len(state_places), sizes.sec * sizes.col
    blocks, refs = refs[:n_blocks], refs[n_blocks:]
    states, refs = refs[:n_states], refs[n_states:]
    tiles, refs = nested(refs[:n_tiles], sizes), refs[n_tiles:]
    inverse_tiles, refs = nested(refs[:n_tiles], sizes), refs[n_tiles:]
    out, up_first, down_first, *refs = refs
    panel, state, rows, left, block_sems, state_sems, tile_sems = refs
    row_index, sec_index, col_index = (lax.axis_index(a) for a in ("row", "sec", "col"))
    count = sizes.chunk

    first_copies = []
    for number, (kx, kc, offset) in enumerate(state_places):
        first = lax.rem(col_index - kc + sizes.col, sizes.col) * sizes.cols + offset
        if kx is not None:
            first = first + lax.rem(sec_index - kx + sizes.sec, sizes.sec) * sizes.width
        height = states[number].shape[0]
        place = state.at[pl.ds(pl.multiple_of(first, height), height)]
        copy = pltpu.make_async_copy(states[number], place, state_sems.at[number])
        first_copies.append((True, copy))
    for number, (ref, row_of) in enumerate(zip(blocks, block_rows)):
        q, low, high = row_of(row_index)
        wanted = (q >= low) & (q <= high)
        source = ref if ref.shape[0] == count else ref.at[part * count : (part + 1) * count]
        begin = pl.multiple_of(jnp.clip(q, 0, sizes.row - 1) * sizes.rows, sizes.rows)
        place = panel.at[:, pl.ds(begin, sizes.rows)]
        first_copies.append((wanted, pltpu.make_async_copy(source, place, block_sems.at[number])))
    start_all(first_copies)
    tile_copies = []
    for number, array in enumerate((tiles, inverse_tiles)):
        tile_copies += chosen_copies(sizes, step, array, rows, number * sizes.rows, tile_sems.at[number])
    start_all(tile_copies)

    wait_all(first_copies)
    image = jnp.dot(panel[...], state[...], preferred_element_type=jnp.float32)
    left[:, : sizes.rows] = image.astype(jnp.bfloat16)
    wait_all(tile_copies)
    begin = col_index * sizes.cols + sec_index * sizes.width + part * count
    inverse_panel = rows[sizes.rows :, pl.ds(pl.multiple_of(begin, count), count)]
    left[:, sizes.rows :] = inverse_panel.T
    for d in range(sizes.row):
        place = lax.rem(d - row_index + sizes.row, sizes.row)
        out[place] = jnp.dot(
            left[...],
            rows[:, d * sizes.rows : (d + 1) * sizes.rows],
            preferred_element_type=jnp.float32,
        )
    up_first[...] = out[sizes.row - 1].astype(jnp.bfloat16)
    down_first[...] = out[1].astype(jnp.bfloat16)


def products(sizes, step, part, blocks, states, tiles, inverse_tiles):
    flat = [tile for per_section in tiles + inverse_tiles for tile in per_section]
    shape = (sizes.row, sizes.chunk, sizes.rows)
    return pl.pallas_call(
        functools.partial(
            products_kernel, sizes, step, part, [b[0] for b in blocks], [s[0] for s in states]
        ),
        out_shape=[jax.ShapeDtypeStruct(shape, jnp.float32)]
        + [jax.ShapeDtypeStruct(shape[1:], jnp.bfloat16)] * 2,
        in_specs=[ANY] * (len(blocks) + len(states) + len(flat)),
        out_specs=[VMEM] * 3,
        scratch_shapes=[
            pltpu.VMEM((sizes.chunk, sizes.order), jnp.bfloat16),
            pltpu.VMEM((sizes.order, sizes.rows), jnp.bfloat16),
            pltpu.VMEM((2 * sizes.rows, sizes.order), jnp.bfloat16),
            pltpu.VMEM((sizes.chunk, 2 * sizes.rows), jnp.bfloat16),
            pltpu.SemaphoreType.DMA((len(blocks),)),
            pltpu.SemaphoreType.DMA((len(states),)),
            pltpu.SemaphoreType.DMA((2, sizes.col)),
        ],
        compiler_params=PARAMS,
        cost_estimate=pl.CostEstimate(
            flops=6 * sizes.rows * sizes.chunk * sizes.order,
            bytes_accessed=6 * sizes.rows * sizes.order + 6 * sizes.chunk * sizes.order,
            transcendentals=0,
        ),
        name="products",
    )(*[b[1] for b in blocks], *[s[1] for s in states], *flat)


def output_kernel(sizes, *refs):
    per_step = sizes.sec * CHUNKS
    out = refs[-1]
    sec_index = lax.axis_index("sec")
    for step in range(sizes.sec):

        @pl.when(sec_index == step)
        def _():
            for kx in range(sizes.sec):
                for k in range(CHUNKS):
                    piece = refs[step * per_step + kx * CHUNKS + k][...]
                    first = lax.rem(sec_index - kx + sizes.sec, sizes.sec) * sizes.width
                    begin = pl.multiple_of(first + k * sizes.chunk, sizes.chunk)
                    out[:, pl.ds(begin, sizes.chunk)] = piece.astype(jnp.float32).T


def output(sizes, pieces):
    return pl.pallas_call(
        functools.partial(output_kernel, sizes),
        out_shape=jax.ShapeDtypeStruct((sizes.rows, sizes.cols), jnp.float32),
        in_specs=[VMEM] * len(pieces),
        out_specs=VMEM,
        compiler_params=PARAMS,
        name="output",
    )(*pieces)


def after(value, *others):
    return lax.optimization_barrier((value, *others))[0]


def neighbours_gathered(sizes, block):
    last = sizes.row - 1
    up = down = block
    found = [(lambda row: (row, 0, last), block)]
    for slot in range(last):
        up = lax.ppermute(up, "row", [(i, i + 1) for i in range(slot, last)])
        down = lax.ppermute(down, "row", [(i, i - 1) for i in range(1, sizes.row - slot)])
        found.append((lambda row, slot=slot: (row - 1 - slot, 0, last), up))
        found.append((lambda row, slot=slot: (row + 1 + slot, 0, last), down))
    return found


def first_slot(sizes, block):
    last = sizes.row - 1
    up = lax.ppermute(block, "row", [(i, i + 1) for i in range(last)])
    down = lax.ppermute(block, "row", [(i, i - 1) for i in range(1, sizes.row)])
    return up, down


def scattered_sum(sizes, partials, gather=None):
    blocks, up_first, down_first = partials
    row_index = lax.axis_index("row")
    last = sizes.row - 1
    up = down = None
    found = []
    for slot in range(last):
        if slot:
            up_block = (blocks[last - slot] + up.astype(jnp.float32)).astype(jnp.bfloat16)
            down_block = (blocks[slot + 1] + down.astype(jnp.float32)).astype(jnp.bfloat16)
        else:
            up_block, down_block = up_first, down_first
        low = slot
        if gather is not None:
            if slot == 0:
                up, down = gather
            if slot < last - 1:
                up_block = jnp.where(row_index <= slot, up_block, up)
                down_block = jnp.where(last - row_index <= slot, down_block, down)
                low = last - 1
        up = lax.ppermute(up_block, "row", [(i, i + 1) for i in range(low + 1)])
        down = lax.ppermute(
            down_block, "row", [(i, i - 1) for i in range(last - low, last + 1)]
        )
        if gather is not None and slot < last - 1:
            found.append((lambda row, slot=slot: (row - 2 - slot, 0, last), up))
            found.append((lambda row, slot=slot: (row + 2 + slot, 0, last), down))
    total = blocks[0] + up.astype(jnp.float32) + down.astype(jnp.float32)
    return total.astype(jnp.bfloat16), found


def local(factors, inverses, sigma_end):
    step_count, rows, cols = factors.shape
    assert step_count == 1
    sizes = Sizes(rows, cols)
    sec_size, col_size, width, chunk = sizes.sec, sizes.col, sizes.width, sizes.chunk
    sec_index = lax.axis_index("sec")

    def panel(tile, offset, part=None):
        first = (sec_index + offset) % sec_size * width
        if part is None:
            return lax.dynamic_slice_in_dim(tile, first, width, 1)
        return lax.dynamic_slice_in_dim(tile, first + part * chunk, chunk, 1)

    factor, inverse = factors[0], inverses[0]

    arrived_chunks = [None]
    for kx in range(1, sec_size):
        arrived_chunks.append(
            [exchanged(panel(factor, kx, part), "sec", kx) for part in range(CHUNKS)]
        )

    factor_blocks = {}
    last = sec_size - 1
    for part in range(CHUNKS):
        sent = [[chunks[part]] for chunks in arrived_chunks[1:]]
        block = transposed_panel(sizes, last, factor, sent, part)
        factor_blocks[last, part] = neighbours_gathered(sizes, block)
    swapped = [chunk for chunks in arrived_chunks[1:] for chunk in chunks]

    def tiles_over_sections(tile, first_chunks):
        found = [tile]
        for kx in range(1, sec_size):
            whole = jnp.zeros_like(tile)
            for j in range(sec_size):
                if j == 0 and first_chunks is not None:
                    piece = jnp.concatenate(first_chunks[kx], axis=1)
                else:
                    piece = exchanged(after(panel(tile, kx + j), *swapped), "sec", kx)
                first = (sec_index + j) % sec_size * width
                whole = lax.dynamic_update_slice_in_dim(whole, piece, first, 1)
            found.append(whole)
        return found

    def over_columns(value):
        return [value] + [exchanged(value, "col", kc) for kc in range(1, col_size)]

    state_pieces = [
        ((None, kc, 0), piece)
        for kc, piece in enumerate(over_columns(sigma_end.astype(jnp.bfloat16).T))
    ]
    factor_tiles = [over_columns(tile) for tile in tiles_over_sections(factor, arrived_chunks)]
    inverse_tiles = [
        over_columns(tile)
        for tile in [inverse]
        + [exchanged(after(inverse, *swapped), "sec", kx) for kx in range(1, sec_size)]
    ]

    results = {}
    for step in reversed(range(sec_size)):
        next_pieces = []
        for part in range(CHUNKS):
            if step:
                earlier = [array for k in range(CHUNKS) for _, array in factor_blocks[step, k][-2:]]
                if part:
                    earlier += partials[1:]
                sent = [[chunks[part]] for chunks in arrived_chunks[1:]]
                block = after(transposed_panel(sizes, step - 1, factor, sent, part), *earlier)
                up, down = first_slot(sizes, block)
            partials = products(
                sizes, step, part, factor_blocks[step, part], state_pieces, factor_tiles, inverse_tiles
            )
            if step:
                total, found = scattered_sum(sizes, partials, (up, down))
                edge = sizes.row - 1
                factor_blocks[step - 1, part] = [
                    (lambda row: (row, 0, edge), block),
                    (lambda row: (row - 1, 0, edge), up),
                    (lambda row: (row + 1, 0, edge), down),
                    *found,
                ]
            else:
                total, _ = scattered_sum(sizes, partials)
            for kx in range(sec_size):
                piece = exchanged(total, "sec", kx) if kx else total
                results[step, kx, part] = piece
                if step:
                    for kc, moved in enumerate(over_columns(piece)):
                        next_pieces.append(((kx, kc, part * chunk), moved))
        state_pieces = next_pieces

    return output(
        sizes,
        [
            results[step, kx, part]
            for step in range(sec_size)
            for kx in range(sec_size)
            for part in range(CHUNKS)
        ],
    )[None]


def solution(mesh):
    in_specs = (
        P(("groups", "sec"), "row", "col"),
        P(("groups", "sec"), "row", "col"),
        P(("groups", "row"), "col"),
    )
    out_specs = P(("groups", "sec"), "row", "col")
    return jax.shard_map(local, mesh=mesh, in_specs=in_specs, out_specs=out_specs, check_vma=False)
```

```python
import functools

import jax
import jax.numpy as jnp
from jax import lax
from jax.experimental import pallas as pl
from jax.experimental.pallas import tpu as pltpu
from jax.sharding import PartitionSpec as P

CHUNKS = 2
ANY = pl.BlockSpec(memory_space=pl.ANY)
VMEM = pl.BlockSpec(memory_space=pltpu.VMEM)
PARAMS = pltpu.CompilerParams(vmem_limit_bytes=12 * 1024 * 1024)


def exchanged(value, axis, steps):
    count = lax.axis_size(axis)
    return lax.ppermute(value, axis, [(i, (i + steps) % count) for i in range(count)])


class Sizes:
    def __init__(self, rows, cols):
        self.row = lax.axis_size("row")
        self.sec = lax.axis_size("sec")
        self.col = lax.axis_size("col")
        self.rows = rows
        self.cols = cols
        self.order = cols * self.col
        self.width = cols // self.sec
        self.chunk = self.width // CHUNKS
        self.per_tile = self.row // self.col


def chosen_copies(sizes, step, tiles, target, top, sems):
    sec_index, col_index = lax.axis_index("sec"), lax.axis_index("col")
    copies = []
    for kc in range(sizes.col):
        begin = lax.rem(col_index - kc + sizes.col, sizes.col) * sizes.cols
        place = target.at[top : top + sizes.rows, pl.ds(pl.multiple_of(begin, sizes.cols), sizes.cols)]
        for kx in range(sizes.sec):
            copy = pltpu.make_async_copy(tiles[kx][kc], place, sems.at[kc])
            wanted = lax.rem(sec_index - kx + sizes.sec, sizes.sec) == step
            copies.append((wanted, copy))
    return copies


def start_all(copies):
    for wanted, copy in copies:
        copy.start() if wanted is True else pl.when(wanted)(copy.start)


def wait_all(copies):
    for wanted, copy in copies:
        copy.wait() if wanted is True else pl.when(wanted)(copy.wait)


def nested(refs, sizes):
    return [refs[kx * sizes.col : (kx + 1) * sizes.col] for kx in range(sizes.sec)]


def panel_kernel(sizes, step, offset, own, *refs):
    *sent, out, held, sem = refs
    sec_index = lax.axis_index("sec")
    count = out.shape[0]
    begin = pl.multiple_of(sec_index * sizes.width + offset, sizes.chunk)
    copies = [(sec_index == step, pltpu.make_async_copy(own.at[:, pl.ds(begin, count)], held, sem))]
    per_section = len(sent) // (sizes.sec - 1)
    for kx in range(1, sizes.sec):
        wanted = lax.rem(sec_index - kx + sizes.sec, sizes.sec) == step
        pieces = sent[(kx - 1) * per_section : kx * per_section]
        height = count // per_section
        for k, piece in enumerate(pieces):
            target = held.at[:, k * height : (k + 1) * height]
            copies.append((wanted, pltpu.make_async_copy(piece, target, sem)))
    start_all(copies)
    wait_all(copies)
    out[...] = held[...].T


def transposed_panel(sizes, step, own, sent, part=None):
    count = sizes.width if part is None else sizes.chunk
    offset = 0 if part is None else part * sizes.chunk
    flat = [piece for pieces in sent for piece in pieces]
    return pl.pallas_call(
        functools.partial(panel_kernel, sizes, step, offset),
        out_shape=jax.ShapeDtypeStruct((count, sizes.rows), jnp.bfloat16),
        in_specs=[pl.BlockSpec(memory_space=pltpu.HBM)] + [VMEM] * len(flat),
        out_specs=VMEM,
        scratch_shapes=[
            pltpu.VMEM((sizes.rows, count), jnp.bfloat16),
            pltpu.SemaphoreType.DMA,
        ],
        compiler_params=PARAMS,
        name="panel",
    )(own, *flat)


def products_kernel(sizes, step, part, block_rows, state_places, *refs):
    n_blocks, n_states, n_tiles = len(block_rows), len(state_places), sizes.sec * sizes.col
    blocks, refs = refs[:n_blocks], refs[n_blocks:]
    states, refs = refs[:n_states], refs[n_states:]
    tiles, refs = nested(refs[:n_tiles], sizes), refs[n_tiles:]
    inverse_tiles, refs = nested(refs[:n_tiles], sizes), refs[n_tiles:]
    out, up_first, down_first, *refs = refs
    panel, state, rows, left, block_sems, state_sems, tile_sems = refs
    row_index, sec_index, col_index = (lax.axis_index(a) for a in ("row", "sec", "col"))
    count = sizes.chunk

    first_copies = []
    for number, (kx, kc, offset) in enumerate(state_places):
        first = lax.rem(col_index - kc + sizes.col, sizes.col) * sizes.cols + offset
        if kx is not None:
            first = first + lax.rem(sec_index - kx + sizes.sec, sizes.sec) * sizes.width
        height = states[number].shape[0]
        place = state.at[pl.ds(pl.multiple_of(first, height), height)]
        copy = pltpu.make_async_copy(states[number], place, state_sems.at[number])
        first_copies.append((True, copy))
    for number, (ref, row_of) in enumerate(zip(blocks, block_rows)):
        q, low, high = row_of(row_index)
        wanted = (q >= low) & (q <= high)
        source = ref if ref.shape[0] == count else ref.at[part * count : (part + 1) * count]
        begin = pl.multiple_of(jnp.clip(q, 0, sizes.row - 1) * sizes.rows, sizes.rows)
        place = panel.at[:, pl.ds(begin, sizes.rows)]
        first_copies.append((wanted, pltpu.make_async_copy(source, place, block_sems.at[number])))
    start_all(first_copies)
    tile_copies = []
    for number, array in enumerate((tiles, inverse_tiles)):
        tile_copies += chosen_copies(sizes, step, array, rows, number * sizes.rows, tile_sems.at[number])
    start_all(tile_copies)

    wait_all(first_copies)
    image = jnp.dot(panel[...], state[...], preferred_element_type=jnp.float32)
    left[:, : sizes.rows] = image.astype(jnp.bfloat16)
    wait_all(tile_copies)
    begin = col_index * sizes.cols + sec_index * sizes.width + part * count
    inverse_panel = rows[sizes.rows :, pl.ds(pl.multiple_of(begin, count), count)]
    left[:, sizes.rows :] = inverse_panel.T
    for d in range(sizes.row):
        place = lax.rem(d - row_index + sizes.row, sizes.row)
        out[place] = jnp.dot(
            left[...],
            rows[:, d * sizes.rows : (d + 1) * sizes.rows],
            preferred_element_type=jnp.float32,
        )
    up_first[...] = out[sizes.row - 1].astype(jnp.bfloat16)
    down_first[...] = out[1].astype(jnp.bfloat16)


def products(sizes, step, part, blocks, states, tiles, inverse_tiles):
    flat = [tile for per_section in tiles + inverse_tiles for tile in per_section]
    shape = (sizes.row, sizes.chunk, sizes.rows)
    return pl.pallas_call(
        functools.partial(
            products_kernel, sizes, step, part, [b[0] for b in blocks], [s[0] for s in states]
        ),
        out_shape=[jax.ShapeDtypeStruct(shape, jnp.float32)]
        + [jax.ShapeDtypeStruct(shape[1:], jnp.bfloat16)] * 2,
        in_specs=[ANY] * (len(blocks) + len(states) + len(flat)),
        out_specs=[VMEM] * 3,
        scratch_shapes=[
            pltpu.VMEM((sizes.chunk, sizes.order), jnp.bfloat16),
            pltpu.VMEM((sizes.order, sizes.rows), jnp.bfloat16),
            pltpu.VMEM((2 * sizes.rows, sizes.order), jnp.bfloat16),
            pltpu.VMEM((sizes.chunk, 2 * sizes.rows), jnp.bfloat16),
            pltpu.SemaphoreType.DMA((len(blocks),)),
            pltpu.SemaphoreType.DMA((len(states),)),
            pltpu.SemaphoreType.DMA((2, sizes.col)),
        ],
        compiler_params=PARAMS,
        cost_estimate=pl.CostEstimate(
            flops=6 * sizes.rows * sizes.chunk * sizes.order,
            bytes_accessed=6 * sizes.rows * sizes.order + 6 * sizes.chunk * sizes.order,
            transcendentals=0,
        ),
        name="products",
    )(*[b[1] for b in blocks], *[s[1] for s in states], *flat)


def output_kernel(sizes, *refs):
    per_step = sizes.sec * CHUNKS
    out = refs[-1]
    sec_index = lax.axis_index("sec")
    for step in range(sizes.sec):

        @pl.when(sec_index == step)
        def _():
            for kx in range(sizes.sec):
                for k in range(CHUNKS):
                    piece = refs[step * per_step + kx * CHUNKS + k][...]
                    first = lax.rem(sec_index - kx + sizes.sec, sizes.sec) * sizes.width
                    begin = pl.multiple_of(first + k * sizes.chunk, sizes.chunk)
                    out[:, pl.ds(begin, sizes.chunk)] = piece.astype(jnp.float32).T


def output(sizes, pieces):
    return pl.pallas_call(
        functools.partial(output_kernel, sizes),
        out_shape=jax.ShapeDtypeStruct((sizes.rows, sizes.cols), jnp.float32),
        in_specs=[VMEM] * len(pieces),
        out_specs=VMEM,
        compiler_params=PARAMS,
        name="output",
    )(*pieces)


def after(value, *others):
    return lax.optimization_barrier((value, *others))[0]


def neighbours_gathered(sizes, block):
    last = sizes.row - 1
    up = down = block
    found = [(lambda row: (row, 0, last), block)]
    for slot in range(last):
        up = lax.ppermute(up, "row", [(i, i + 1) for i in range(slot, last)])
        down = lax.ppermute(down, "row", [(i, i - 1) for i in range(1, sizes.row - slot)])
        found.append((lambda row, slot=slot: (row - 1 - slot, 0, last), up))
        found.append((lambda row, slot=slot: (row + 1 + slot, 0, last), down))
    return found


def first_slot(sizes, block):
    last = sizes.row - 1
    up = lax.ppermute(block, "row", [(i, i + 1) for i in range(last)])
    down = lax.ppermute(block, "row", [(i, i - 1) for i in range(1, sizes.row)])
    return up, down


def scattered_sum(sizes, partials, gather=None):
    blocks, up_first, down_first = partials
    row_index = lax.axis_index("row")
    last = sizes.row - 1
    up = down = None
    found = []
    for slot in range(last):
        if slot:
            up_block = (blocks[last - slot] + up.astype(jnp.float32)).astype(jnp.bfloat16)
            down_block = (blocks[slot + 1] + down.astype(jnp.float32)).astype(jnp.bfloat16)
        else:
            up_block, down_block = up_first, down_first
        low = slot
        if gather is not None:
            if slot == 0:
                up, down = gather
            if slot < last - 1:
                up_block = jnp.where(row_index <= slot, up_block, up)
                down_block = jnp.where(last - row_index <= slot, down_block, down)
                low = last - 1
        up = lax.ppermute(up_block, "row", [(i, i + 1) for i in range(low + 1)])
        down = lax.ppermute(
            down_block, "row", [(i, i - 1) for i in range(last - low, last + 1)]
        )
        if gather is not None and slot < last - 1:
            found.append((lambda row, slot=slot: (row - 2 - slot, 0, last), up))
            found.append((lambda row, slot=slot: (row + 2 + slot, 0, last), down))
    total = blocks[0] + up.astype(jnp.float32) + down.astype(jnp.float32)
    return total.astype(jnp.bfloat16), found


def local(factors, inverses, sigma_end):
    step_count, rows, cols = factors.shape
    assert step_count == 1
    sizes = Sizes(rows, cols)
    sec_size, col_size, width, chunk = sizes.sec, sizes.col, sizes.width, sizes.chunk
    sec_index = lax.axis_index("sec")

    def panel(tile, offset, part=None):
        first = (sec_index + offset) % sec_size * width
        if part is None:
            return lax.dynamic_slice_in_dim(tile, first, width, 1)
        return lax.dynamic_slice_in_dim(tile, first + part * chunk, chunk, 1)

    factor, inverse = factors[0], inverses[0]

    arrived_chunks = [None]
    for kx in range(1, sec_size):
        arrived_chunks.append(
            [exchanged(panel(factor, kx, part), "sec", kx) for part in range(CHUNKS)]
        )

    factor_blocks = {}
    last = sec_size - 1
    for part in range(CHUNKS):
        sent = [[chunks[part]] for chunks in arrived_chunks[1:]]
        block = transposed_panel(sizes, last, factor, sent, part)
        factor_blocks[last, part] = neighbours_gathered(sizes, block)
    swapped = [chunk for chunks in arrived_chunks[1:] for chunk in chunks]

    def tiles_over_sections(tile, first_chunks):
        found = [tile]
        for kx in range(1, sec_size):
            whole = jnp.zeros_like(tile)
            for j in range(sec_size):
                if j == 0 and first_chunks is not None:
                    piece = jnp.concatenate(first_chunks[kx], axis=1)
                else:
                    piece = exchanged(after(panel(tile, kx + j), *swapped), "sec", kx)
                first = (sec_index + j) % sec_size * width
                whole = lax.dynamic_update_slice_in_dim(whole, piece, first, 1)
            found.append(whole)
        return found

    def over_columns(value):
        return [value] + [exchanged(value, "col", kc) for kc in range(1, col_size)]

    state_pieces = [
        ((None, kc, 0), piece)
        for kc, piece in enumerate(over_columns(sigma_end.astype(jnp.bfloat16).T))
    ]
    factor_tiles = [over_columns(tile) for tile in tiles_over_sections(factor, arrived_chunks)]
    inverse_tiles = [
        over_columns(tile)
        for tile in [inverse]
        + [exchanged(after(inverse, *swapped), "sec", kx) for kx in range(1, sec_size)]
    ]

    results = {}
    for step in reversed(range(sec_size)):
        next_pieces = []
        for part in range(CHUNKS):
            if step:
                earlier = [array for k in range(CHUNKS) for _, array in factor_blocks[step, k][-2:]]
                if part:
                    earlier += partials[1:]
                sent = [[chunks[part]] for chunks in arrived_chunks[1:]]
                block = after(transposed_panel(sizes, step - 1, factor, sent, part), *earlier)
                up, down = first_slot(sizes, block)
            partials = products(
                sizes, step, part, factor_blocks[step, part], state_pieces, factor_tiles, inverse_tiles
            )
            if step:
                total, found = scattered_sum(sizes, partials, (up, down))
                edge = sizes.row - 1
                factor_blocks[step - 1, part] = [
                    (lambda row: (row, 0, edge), block),
                    (lambda row: (row - 1, 0, edge), up),
                    (lambda row: (row + 1, 0, edge), down),
                    *found,
                ]
            else:
                total, _ = scattered_sum(sizes, partials)
            for kx in range(sec_size):
                piece = exchanged(total, "sec", kx) if kx else total
                results[step, kx, part] = piece
                if step:
                    for kc, moved in enumerate(over_columns(piece)):
                        next_pieces.append(((kx, kc, part * chunk), moved))
        state_pieces = next_pieces

    return output(
        sizes,
        [
            results[step, kx, part]
            for step in range(sec_size)
            for kx in range(sec_size)
            for part in range(CHUNKS)
        ],
    )[None]


def solution(mesh):
    in_specs = (
        P(("groups", "sec"), "row", "col"),
        P(("groups", "sec"), "row", "col"),
        P(("groups", "row"), "col"),
    )
    out_specs = P(("groups", "sec"), "row", "col")
    return jax.shard_map(local, mesh=mesh, in_specs=in_specs, out_specs=out_specs, check_vma=False)
```
